128 devices in a mesh: gx: 8 (over z, core), gy: 16 (over x, y).
Axes of the slice: x: 4, y: 4, z: 4, core: 2. Of those that a mesh axis runs over, the one named last changes fastest.
Arguments:
- gaseous_rho: float32 [16, 1536, 1024], P(None, 'gy', 'gx'), may hold values from 0.5 to 2
- gaseous_flow_vector: float32 [3, 16, 1536, 1024], P(None, None, 'gy', 'gx'), may hold values from -1 to 1
- gaseous_kelvin: float32 [16, 1536, 1024], P(None, 'gy', 'gx'), may hold values from 0.5 to 2
- sender_tile_map: int32 [128, 256], P(('gx', 'gy')), may hold values from -1 to 1535, as said below
- receiver_arrival_rank: int32 [8192], P(('gx', 'gy')), may hold values from -1 to 255, as said below
- bin_active_number: int32 [8192], P(('gx', 'gy')), may hold values from 0 to 512, as said below
- grain_inertia: float32 [8192, 512], P(('gx', 'gy')), may hold values from 0.05 to 0.5
- grain_motion_vector: float32 [3, 8192, 512], P(None, ('gx', 'gy')), may hold values from -5 to 5
- grain_kelvin: float32 [8192, 512], P(('gx', 'gy')), may hold values from 0.5 to 4
- grain_voxel_number: int32 [8192, 512], P(('gx', 'gy')), may hold values from 0 to 127
- grain_substance_label: int32 [8192, 512], P(('gx', 'gy')), may hold values from 0 to 1
- exchange_factor: float32 [2, 2], replicated, may hold values from 0.5 to 4
Outputs:
- gas_state_out: float32 [5, 16, 1536, 1024], P(None, None, 'gy', 'gx')
- solid_state: float32 [4, 8192, 2, 128], P(None, ('gx', 'gy'))
The draws below stay inside these ranges and needn't reach their ends.
Inputs may be any that keep to these rules, and one draw needn't show every extreme that they name: sender_tile_map[s, o * 2 + r] is the local block that device s sends as its r-th block to owner o, -1 where it sends fewer; the blocks of one device are distinct; only 32 devices send, each to every owner. `receiver_arrival_rank`: an owner's live slots come first, 48 or more of them, and name each sent block of that owner once; in each draw some owner has all 64 live and receives exactly 2 blocks from each sending device. `bin_active_number`: 0 exactly on slots with receiver_arrival_rank -1, else 512 // 2 or more; some slot holds 512.
All inputs are finite; a program needn't handle non-finite values.
Results may differ from the reference program's by a relative error of at most 0.0003.
Values sent between devices are 32-bit elements; how exact they have to be, the bound alone decides.
No kernel may reach another device: no remote copies, remote signals or barrier semaphores. Data moves between devices by JAX's collectives and lax.ppermute only.
A program may use at most 128 MiB of HBM per device.

```python
import math
import jax
import jax.numpy as jnp
from jax import lax

CX = 128
CY = 96
CZ = 16
SLOTS = 64
BIN_CAPACITY = 512
CAP = 2
GRID_WIDTH_EAST = 1024
GRID_WIDTH_NORTH = 1536
GRID_WIDTH_UPWARD = 16
RECEIVER_BINS = 8192
N_GX = 8
N_GY = 16


def first_last(order, length):
    positions = jnp.arange(length)
    last = length - 1
    return jnp.where(positions == 0, last, jnp.where(order == last, order[0], order))


def shuffle(subkey):
    return first_last(jax.random.permutation(subkey, CZ * CY), CZ * CY)


def routing(key):
    devices = N_GX * N_GY
    hot_count = devices // 4
    capacity = 4 * SLOTS // devices
    subkeys = jax.random.split(key, 6)
    filled = jax.random.randint(subkeys[0], (devices,), 3 * SLOTS // 4, SLOTS + 1)
    fullest = jax.random.randint(subkeys[1], (), 0, devices)
    filled = filled.at[(fullest + 1) % devices].set(3 * SLOTS // 4)
    filled = filled.at[fullest].set(SLOTS)
    offset = jax.random.randint(subkeys[2], (devices,), 0, hot_count)
    hot_devices = first_last(jax.random.permutation(subkeys[3], devices), devices)[:hot_count]
    position = jnp.arange(SLOTS)[None, :]
    present = position < filled[:, None]
    source = hot_devices[(position + offset[:, None]) % hot_count]
    queue_rank = position // hot_count
    receiver_arrival_rank = jnp.where(present, source * capacity + queue_rank, -1)
    orders = jax.vmap(shuffle)(jax.random.split(subkeys[4], devices))
    owner_index = jnp.arange(devices)[:, None]
    column = owner_index * capacity + queue_rank
    chosen = orders[source, column].astype(jnp.int32)
    send_rows = jnp.full((devices, devices * capacity), -1, jnp.int32)
    send_rows = send_rows.at[jnp.where(present, source, devices), column].set(chosen, mode='drop')
    counts = jax.random.randint(subkeys[5], (devices, SLOTS), BIN_CAPACITY // 2, BIN_CAPACITY + 1)
    counts = counts.at[fullest, 0].set(BIN_CAPACITY)
    counts = jnp.where(present, counts, 0)
    return (send_rows, receiver_arrival_rank.reshape(-1).astype(jnp.int32), counts.reshape(-1).astype(jnp.int32))


def draw_sender_tile_map(key, part):
    return routing(key)[0]


def draw_receiver_arrival_rank(key, part):
    return routing(key)[1]


def draw_bin_active_number(key, part):
    return routing(key)[2]


def with_ends(result, key, smallest, high):
    dims = result.shape
    spot = [jax.random.randint(jax.random.fold_in(key, axis), (), 0, dims[axis]) for axis in range(len(dims))]
    result = result.at[tuple(spot)].set(smallest)
    longest = dims.index(max(dims))
    spot[longest] = (spot[longest] + 1) % dims[longest]
    return result.at[tuple(spot)].set(high)


def block_scale(own_key, extent, cuts, smallest, high):
    def one(dim, parts):
        draws = jax.random.uniform(jax.random.fold_in(jax.random.fold_in(own_key, 6), dim), (parts,), jnp.float32, smallest / len(cuts), high / len(cuts))
        return jnp.repeat(jnp.exp(draws), extent[dim] // parts).reshape((-1,) + (1,) * (len(extent) - dim - 1))

    loudness = one(*cuts[0])
    for cut in cuts[1:]:
        loudness = loudness * one(*cut)
    return loudness


def centred(stream_key, shape, deviation, bound, cuts=(), dtype=jnp.bfloat16):
    result = deviation * jax.random.normal(stream_key, shape, jnp.float32)
    if cuts:
        result = result * block_scale(stream_key, shape, cuts, -0.22, 0.18)
    return jnp.clip(result, -bound, bound).astype(dtype)


def setup_inputs(seed: int = 0) -> dict:
    arg_keys = jax.random.split(jax.random.key(seed), 13)
    gaseous_rho = jnp.clip(0.5 + 1.5 * jax.random.uniform(arg_keys[0], (GRID_WIDTH_UPWARD, GRID_WIDTH_NORTH, GRID_WIDTH_EAST), jnp.float32) ** block_scale(arg_keys[0], (GRID_WIDTH_UPWARD, GRID_WIDTH_NORTH, GRID_WIDTH_EAST), ((1, 16), (2, 8)), -0.2, 0.2), 0.5, 2.0)
    gaseous_flow_vector = jnp.clip(jax.random.uniform(arg_keys[1], (3, GRID_WIDTH_UPWARD, GRID_WIDTH_NORTH, GRID_WIDTH_EAST), jnp.float32, -1.0, 1.0) * block_scale(arg_keys[1], (3, GRID_WIDTH_UPWARD, GRID_WIDTH_NORTH, GRID_WIDTH_EAST), ((2, 16), (3, 8)), -0.4, 0.0), -1.0, 1.0)
    gaseous_kelvin = jnp.clip(0.5 + 1.5 * jax.random.uniform(arg_keys[2], (GRID_WIDTH_UPWARD, GRID_WIDTH_NORTH, GRID_WIDTH_EAST), jnp.float32) ** block_scale(arg_keys[2], (GRID_WIDTH_UPWARD, GRID_WIDTH_NORTH, GRID_WIDTH_EAST), ((1, 16), (2, 8)), -0.2, 0.2), 0.5, 2.0)
    sender_tile_map = draw_sender_tile_map(jax.random.fold_in(arg_keys[12], 71), 0)
    receiver_arrival_rank = draw_receiver_arrival_rank(jax.random.fold_in(arg_keys[12], 71), 0)
    bin_active_number = draw_bin_active_number(jax.random.fold_in(arg_keys[12], 71), 0)
    grain_inertia = jnp.clip(jnp.exp(math.log(0.5) - 2.3025851 * jax.random.uniform(arg_keys[6], (RECEIVER_BINS, BIN_CAPACITY), jnp.float32) ** block_scale(arg_keys[6], (RECEIVER_BINS, BIN_CAPACITY), ((0, 128),), -0.2, 0.2)), 0.05, 0.5)
    grain_motion_vector = centred(arg_keys[7], (3, RECEIVER_BINS, BIN_CAPACITY), 1.0, 5.0, ((1, 128),), jnp.float32)
    grain_kelvin = jnp.clip(0.5 + 3.5 * jax.random.uniform(arg_keys[8], (RECEIVER_BINS, BIN_CAPACITY), jnp.float32) ** block_scale(arg_keys[8], (RECEIVER_BINS, BIN_CAPACITY), ((0, 128),), -0.2, 0.2), 0.5, 4.0)
    grain_voxel_number = with_ends(jax.random.randint(arg_keys[9], (RECEIVER_BINS, BIN_CAPACITY), 0, CX), jax.random.fold_in(arg_keys[9], 1), 0, CX - 1).astype(jnp.int32)
    grain_substance_label = with_ends(jax.random.randint(arg_keys[10], (RECEIVER_BINS, BIN_CAPACITY), 0, 2), jax.random.fold_in(arg_keys[10], 1), 0, 1).astype(jnp.int32)
    exchange_factor = jnp.clip(jnp.exp(jax.random.uniform(arg_keys[11], (2, 2), jnp.float32, math.log(0.5), math.log(4.0))), 0.5, 4.0)
    return dict(gaseous_rho=gaseous_rho, gaseous_flow_vector=gaseous_flow_vector, gaseous_kelvin=gaseous_kelvin, sender_tile_map=sender_tile_map, receiver_arrival_rank=receiver_arrival_rank, bin_active_number=bin_active_number, grain_inertia=grain_inertia, grain_motion_vector=grain_motion_vector, grain_kelvin=grain_kelvin, grain_voxel_number=grain_voxel_number, grain_substance_label=grain_substance_label, exchange_factor=exchange_factor)


step_ratio = 0.08


def edge_mask(length):
    positions = jnp.arange(length + 1)
    return (positions == 0) | (positions == length)


def face_pair(quantity_array, direction):
    ndims = quantity_array.ndim
    lower_index = [slice(None)] * (ndims - 3) + [slice(1, -1)] * 3
    upper_index = list(lower_index)
    lower_index[ndims - 3 + direction] = slice(0, -1)
    upper_index[ndims - 3 + direction] = slice(1, None)
    return quantity_array[tuple(lower_index)], quantity_array[tuple(upper_index)]


def advance(padded, wall_masks):
    density = padded[0]
    pressure = padded[0] * padded[4]
    conserved = jnp.concatenate([padded[0:1], padded[0:1] * padded[1:4], padded[0:1] * padded[4:5]], 0)
    change = 0.0
    for direction in range(3):
        dens_lower, dens_upper = face_pair(density, direction)
        press_lower, press_upper = face_pair(pressure, direction)
        normal_lower, normal_upper = face_pair(padded[3 - direction], direction)
        face_speed = 0.5 * (normal_lower + normal_upper) - step_ratio * (press_upper - press_lower) * 2.0 / (dens_lower + dens_upper)
        mask_shape = [1, 1, 1]
        mask_shape[direction] = -1
        face_speed = jnp.where(wall_masks[direction].reshape(mask_shape), 0.0, face_speed)
        cons_lower, cons_upper = face_pair(conserved, direction)
        face_flux = face_speed * jnp.where(face_speed > 0, cons_lower, cons_upper)
        count_faces = face_flux.shape[1 + direction]
        change = change + lax.slice_in_dim(face_flux, 1, count_faces, axis=1 + direction) - lax.slice_in_dim(face_flux, 0, count_faces - 1, axis=1 + direction)
    central = conserved[:, 1:-1, 1:-1, 1:-1]
    updated = central - step_ratio * change
    return jnp.concatenate([updated[0:1], updated[1:4] / updated[0:1], updated[4:5] / updated[0:1]], 0)


def grain_quantities(grain_inertia, grain_motion_vector, grain_kelvin, bin_active_number):
    padding = grain_inertia.shape[1]
    present = jnp.arange(padding)[None, :] < bin_active_number[:, None]
    inertia_scaled = jnp.where(present, grain_inertia, 0.0)
    return jnp.stack([inertia_scaled, inertia_scaled * grain_motion_vector[0], inertia_scaled * grain_motion_vector[1], inertia_scaled * grain_motion_vector[2], inertia_scaled * grain_kelvin], 0)


def couple(gas, grid, exchange_factor):
    gaseous_inertia = gas[0]
    gaseous_motion = gas[1:4]
    gaseous_enthalpy = gas[4]
    rigid_inertia = grid[0]
    solid_momentum = grid[1:4]
    rigid_enthalpy = grid[4]
    drag = exchange_factor[:, 0][None, :, None]
    thermal_coupler = exchange_factor[:, 1][None, :, None]
    drag_total = rigid_inertia + drag
    next_flow_vector = (gaseous_inertia * gaseous_motion + jnp.sum(drag * solid_momentum / drag_total, axis=2)) / (gaseous_inertia + jnp.sum(drag * rigid_inertia / drag_total, axis=1))
    rigid_motion_vector = (solid_momentum + drag * next_flow_vector[:, :, None, :]) / drag_total
    summed_enthalpy = rigid_inertia + thermal_coupler
    next_kelvin = (gaseous_inertia * gaseous_enthalpy + jnp.sum(thermal_coupler * rigid_enthalpy / summed_enthalpy, axis=1)) / (gaseous_inertia + jnp.sum(thermal_coupler * rigid_inertia / summed_enthalpy, axis=1))
    rigid_kelvin = (rigid_enthalpy + thermal_coupler * next_kelvin[:, None, :]) / summed_enthalpy
    increment_changes = jnp.concatenate([next_flow_vector - gaseous_motion, (next_kelvin - gaseous_enthalpy)[None]], 0)
    rigid_constituent = jnp.concatenate([rigid_motion_vector, rigid_kelvin[None]], 0)
    return increment_changes, rigid_constituent


def reference(gaseous_rho, gaseous_flow_vector, gaseous_kelvin, sender_tile_map, receiver_arrival_rank, bin_active_number, grain_inertia, grain_motion_vector, grain_kelvin, grain_voxel_number, grain_substance_label, exchange_factor):
    voxel_record = jnp.concatenate([gaseous_rho[None], gaseous_flow_vector, gaseous_kelvin[None]], 0)
    padded = jnp.pad(voxel_record, ((0, 0), (1, 1), (1, 1), (1, 1)))
    advanced = advance(padded, [edge_mask(GRID_WIDTH_UPWARD), edge_mask(GRID_WIDTH_NORTH), edge_mask(GRID_WIDTH_EAST)])
    devices = N_GX * N_GY
    blocks = advanced.reshape(5, GRID_WIDTH_UPWARD, N_GY, CY, N_GX, CX).transpose(0, 4, 2, 1, 3, 5).reshape(5, devices, GRID_WIDTH_UPWARD * CY, CX)
    slot_owner = jnp.arange(RECEIVER_BINS) // SLOTS
    live_slot = receiver_arrival_rank >= 0
    safe_source = jnp.maximum(receiver_arrival_rank, 0)
    source_device = safe_source // CAP
    source_rank = safe_source % CAP
    local_block = sender_tile_map[source_device, slot_owner * CAP + source_rank]
    gas = blocks[:, source_device, local_block]
    quantity_array = grain_quantities(grain_inertia, grain_motion_vector, grain_kelvin, bin_active_number)
    target = (jnp.arange(RECEIVER_BINS)[:, None] * 2 + grain_substance_label) * CX + grain_voxel_number
    summed = jax.ops.segment_sum(quantity_array.reshape(5, -1).T, target.reshape(-1), num_segments=RECEIVER_BINS * 2 * CX)
    grid = summed.T.reshape(5, RECEIVER_BINS, 2, CX)
    increment_changes, rigid_constituent = couple(gas, grid, exchange_factor)
    target_device = jnp.where(live_slot, source_device, devices)
    gains = jnp.zeros_like(blocks[1:]).at[:, target_device, local_block].add(increment_changes, mode="drop")
    final = jnp.concatenate([blocks[0:1], blocks[1:] + gains], 0)
    gas_state_out = final.reshape(5, N_GX, N_GY, GRID_WIDTH_UPWARD, CY, CX).transpose(0, 3, 2, 4, 1, 5).reshape(5, GRID_WIDTH_UPWARD, GRID_WIDTH_NORTH, GRID_WIDTH_EAST)
    solid_state = jnp.where(live_slot[None, :, None, None], rigid_constituent, 0.0)
    return gas_state_out, solid_state
```

```python
import functools
import jax
import jax.numpy as jnp
from jax import lax
from jax.experimental import pallas as pl
from jax.experimental.pallas import tpu as pltpu
from jax.sharding import PartitionSpec as P

step_ratio = 0.08
fields = 5
lanes = 128
row_pad = 8
block_rows = 12
gas_row = 6
row_chunk = 16

VM = pltpu.VMEM
vmem_spec = pl.BlockSpec(memory_space=pltpu.VMEM)
smem_spec = pl.BlockSpec(memory_space=pltpu.SMEM)
any_spec = pl.BlockSpec(memory_space=pl.ANY)


def params(mib):
    return pltpu.CompilerParams(vmem_limit_bytes=mib * 1024 * 1024)


def struct(*shape):
    return jax.ShapeDtypeStruct(shape, jnp.float32)


def lane_index(shape):
    return lax.broadcasted_iota(jnp.int32, shape, len(shape) - 1)


def edges_kernel(rho, flow, kelvin, left, right, low, high, held, sems):
    depth, height, _ = rho.shape
    parts = sems.shape[1]
    rows = height // parts

    def copies(part):
        span = pl.ds(part * rows, rows)
        return [
            pltpu.make_async_copy(rho.at[:, span], held.at[0, :, span], sems.at[0, part]),
            pltpu.make_async_copy(flow.at[:, :, span], held.at[1:4, :, span], sems.at[1, part]),
            pltpu.make_async_copy(kelvin.at[:, span], held.at[4, :, span], sems.at[2, part]),
        ]

    for part in range(parts):
        for copy in copies(part):
            copy.start()
    lane = lane_index((8, lanes))
    for part in range(parts):
        for copy in copies(part):
            copy.wait()

        def group(g, carry):
            start = pl.multiple_of(part * rows + g * 8, 8)
            span = pl.ds(start, 8)
            first = jnp.zeros((8, lanes), jnp.float32)
            last = jnp.zeros((8, lanes), jnp.float32)
            for f in range(fields):
                for z in range(depth):
                    k = f * depth + z
                    turned = pltpu.roll(held[f, z, span, :], k + 1, 1)
                    last = jnp.where(lane == k, turned, last)
                    first = jnp.where(lane == k + 1, turned, first)
            left[span, :] = pltpu.roll(first, lanes - 1, 1)
            right[span, :] = last
            return carry

        lax.fori_loop(0, rows // 8, group, 0)
    for f in range(fields):
        for z in range(depth):
            k = f * depth + z
            low[k : k + 1, :] = held[f, z, 0:1, :]
            high[k : k + 1, :] = held[f, z, height - 1 : height, :]


def edges(rho, flow, kelvin):
    depth, height, width = rho.shape
    parts = 4
    return pl.pallas_call(
        edges_kernel,
        out_shape=(
            struct(height, width),
            struct(height, width),
            struct(fields * depth, width),
            struct(fields * depth, width),
        ),
        in_specs=[any_spec] * 3,
        out_specs=(vmem_spec,) * 4,
        scratch_shapes=[
            VM((fields, depth, height, width), jnp.float32),
            pltpu.SemaphoreType.DMA((3, parts)),
        ],
        compiler_params=params(24),
        name="edges",
    )(rho, flow, kelvin)


def binning_kernel(count, factor, mass, flow, kelvin, cell, label, shared, solid, held, sums):
    slots, padding = mass.shape
    width = lanes

    def group(g, carry):
        span = pl.ds(pl.multiple_of(g * 8, 8), 8)
        base = pl.multiple_of(g * 64, 64)
        for part in range(padding // lanes):
            chunk = pl.ds(part * lanes, lanes)
            m = mass[span, chunk]
            values = [m] + [m * flow[c, span, chunk] for c in range(3)] + [m * kelvin[span, chunk]]
            values = values + [jnp.zeros_like(m)] * 3
            for c in range(8):
                held[part, pl.ds(base + c, 8, stride=8), :] = values[c]
        return carry

    lax.fori_loop(0, slots // 8, group, 0)
    place = lane_index((1, padding))
    columns = lax.broadcasted_iota(jnp.int32, (width, padding), 0)

    def slot_sums(s, carry):
        row = pl.ds(pl.multiple_of(s * 8, 8), 8)
        base = jnp.concatenate([held[part, row, :] for part in range(padding // lanes)], 1)
        target = jnp.where(place < count[s], cell[pl.ds(s, 1), :], -1)
        kind = label[pl.ds(s, 1), :]
        table = jnp.where(columns == target, 1.0, 0.0).astype(jnp.bfloat16)
        both = jnp.concatenate(
            [jnp.where(kind == 0, base, 0.0), jnp.where(kind == 1, base, 0.0)], 0
        )
        coarse = both.astype(jnp.bfloat16)
        fine = (both - coarse.astype(jnp.float32)).astype(jnp.bfloat16)
        summed = lax.dot_general(
            jnp.concatenate([coarse, fine], 0),
            table,
            (((1,), (1,)), ((), ())),
            preferred_element_type=jnp.float32,
        )
        sums[pl.ds(pl.multiple_of(s * 16, 16), 16), :] = summed[0:16] + summed[16:32]
        return carry

    lax.fori_loop(0, slots, slot_sums, 0, unroll=4)
    totals = [0.0] * 6
    for m in range(2):
        drag, thermal = factor[m, 0], factor[m, 1]

        def row(c):
            return sums[pl.ds(8 * m + c, slots, stride=16), :]

        inertia = row(0)
        by_drag = 1.0 / (inertia + drag)
        by_heat = 1.0 / (inertia + thermal)
        for c in range(3):
            scaled = row(1 + c) * by_drag
            solid[(m * 6 + c) * slots : (m * 6 + c + 1) * slots, :] = scaled
            totals[c] = totals[c] + drag * scaled
        scaled = row(4) * by_heat
        solid[(m * 6 + 3) * slots : (m * 6 + 4) * slots, :] = scaled
        totals[3] = totals[3] + thermal * scaled
        by_drag = drag * by_drag
        by_heat = thermal * by_heat
        solid[(m * 6 + 4) * slots : (m * 6 + 5) * slots, :] = by_drag
        solid[(m * 6 + 5) * slots : (m * 6 + 6) * slots, :] = by_heat
        totals[4] = totals[4] + by_drag * inertia
        totals[5] = totals[5] + by_heat * inertia
    for c in range(6):
        shared[c * slots : (c + 1) * slots, :] = totals[c]


def binning(count, factor, mass, flow, kelvin, cell, label):
    slots, padding = mass.shape
    return pl.pallas_call(
        binning_kernel,
        out_shape=(struct(6 * slots, lanes), struct(12 * slots, lanes)),
        in_specs=[smem_spec] * 2 + [vmem_spec] * 5,
        out_specs=(vmem_spec,) * 2,
        scratch_shapes=[
            VM((padding // lanes, slots * 8, lanes), jnp.float32),
            VM((slots * 16, lanes), jnp.float32),
        ],
        cost_estimate=pl.CostEstimate(
            flops=4_000_000_000, bytes_accessed=12_000_000, transcendentals=0
        ),
        compiler_params=params(16),
        name="binning",
    )(count, factor, mass, flow, kelvin, cell, label)


def fluxes(a, b, normal, keep=None):
    speed = (0.5 * step_ratio) * (a[normal] + b[normal]) - (2.0 * step_ratio * step_ratio) * (
        b[0] * b[4] - a[0] * a[4]
    ) / (a[0] + b[0])
    if keep is not None:
        speed = speed * keep
    ahead = speed > 0
    chosen = [jnp.where(ahead, u, v) for u, v in zip(a, b)]
    through = speed * chosen[0]
    return [through] + [through * c for c in chosen[1:]]


def advect_kernel(
    tiles,
    rank,
    rho,
    flow,
    kelvin,
    own_left,
    own_right,
    from_left,
    from_right,
    from_low,
    from_high,
    shared,
    gas_out,
    send_out,
    state,
    gas,
    send,
    flux_z,
    flux_y,
    side,
    in_sems,
    out_sems,
    send_sem,
):
    depth, height, width = rho.shape
    cells = depth * height
    slots = rank.shape[0]
    gx, gy = lax.axis_index("gx"), lax.axis_index("gy")

    def keep(wall):
        return jnp.where(wall, 0.0, 1.0).astype(jnp.float32)

    keep_left = keep(gx == 0)
    keep_right = keep(gx == lax.axis_size("gx") - 1)
    keep_low = keep(gy == 0)
    keep_high = keep(gy == lax.axis_size("gy") - 1)
    inner = pl.ds(row_pad, height)

    def loads(z):
        return [
            pltpu.make_async_copy(rho.at[z], state.at[0, z, inner], in_sems.at[0, z]),
            pltpu.make_async_copy(flow.at[:, z], state.at[1:4, z, inner], in_sems.at[1, z]),
            pltpu.make_async_copy(kelvin.at[z], state.at[4, z, inner], in_sems.at[2, z]),
        ]

    def store(z):
        rows = pl.ds(pl.multiple_of(z * height, 8), height)
        return pltpu.make_async_copy(gas.at[:, rows], gas_out.at[:, z], out_sems.at[z])

    def start_loads(z, carry):
        for copy in loads(z):
            copy.start()
        return carry

    lax.fori_loop(0, depth, start_loads, 0)

    def boundary(g, carry):
        span = pl.ds(pl.multiple_of(g * 8, 8), 8)

        def split(ref):
            packed = ref[span, :]
            return [packed] + [
                pltpu.roll(packed, lanes - f * depth, 1) for f in range(1, fields)
            ]

        lower = fluxes(split(from_left), split(own_left), 1, keep_left)
        upper = fluxes(split(own_right), split(from_right), 1, keep_right)
        for f in range(fields):
            side[f, span, :] = lower[f]
            side[fields + f, span, :] = upper[f]
        return carry

    lax.fori_loop(0, height // 8, boundary, 0)

    for f in range(fields):
        flux_z[f] = jnp.zeros((height, width), jnp.float32)
    for copy in loads(0):
        copy.wait()
    lane = lane_index((row_chunk, lanes))

    def plane(z, carry):
        above = jnp.minimum(z + 1, depth - 1)

        @pl.when(z + 1 < depth)
        def _():
            for copy in loads(above):
                copy.wait()

        keep_z = keep(z + 1 == depth)
        for f in range(fields):
            k = f * depth + z
            state[f, z, row_pad - 1 : row_pad, :] = from_low[pl.ds(k, 1), :]
            state[f, z, row_pad + height : row_pad + height + 1, :] = from_high[pl.ds(k, 1), :]

        def faces_y(start, rows):
            a = [state[f, z, pl.ds(row_pad - 1 + start, rows), :] for f in range(fields)]
            b = [state[f, z, pl.ds(row_pad + start, rows), :] for f in range(fields)]
            for f, value in enumerate(fluxes(a, b, 2)):
                flux_y[f, start : start + rows, :] = value

        for start in range(0, height, row_chunk):
            faces_y(start, row_chunk)
        faces_y(height, 1)
        for f in range(fields):
            flux_y[f, 0:1, :] = flux_y[f, 0:1, :] * keep_low
            flux_y[f, height : height + 1, :] = flux_y[f, height : height + 1, :] * keep_high

        for start in range(0, height, row_chunk):
            span = pl.ds(start, row_chunk)
            here = [state[f, z, pl.ds(row_pad + start, row_chunk), :] for f in range(fields)]
            over = [state[f, above, pl.ds(row_pad + start, row_chunk), :] for f in range(fields)]
            up = fluxes(here, over, 3, keep_z)
            change = []
            for f in range(fields):
                change.append(
                    (up[f] - flux_z[f, span, :])
                    + (flux_y[f, pl.ds(start + 1, row_chunk), :] - flux_y[f, span, :])
                )
                flux_z[f, span, :] = up[f]
            before = [pltpu.roll(h, 1, 1) for h in here]
            faces = fluxes(before, here, 1)
            for f in range(fields):
                lower = pltpu.roll(side[f, span, :], lanes - z, 1)
                upper = pltpu.roll(side[fields + f, span, :], lanes - 1 - z, 1)
                face = jnp.where(lane == 0, lower, faces[f])
                after = jnp.where(lane == lanes - 1, upper, pltpu.roll(face, lanes - 1, 1))
                change[f] = change[f] + (after - face)
            density = here[0] - change[0]
            inverse = 1.0 / density
            rows = pl.ds(pl.multiple_of(z * height + start, 8), row_chunk)
            gas[0, rows, :] = density
            for f in range(1, fields):
                gas[f, rows, :] = (here[0] * here[f] - change[f]) * inverse
        store(z).start()
        return carry

    lax.fori_loop(0, depth, plane, 0)

    total = tiles.shape[1]

    def pack_gas(i, carry):
        block = jnp.maximum(tiles[0, i], 0)
        for f in range(fields):
            send[pl.ds(i * block_rows + gas_row + f, 1), :] = gas[f, pl.ds(block, 1), :]
        return carry

    lax.fori_loop(0, total, pack_gas, 0, unroll=8)

    def pack_shared(k, carry):
        where_to = rank[k]
        row = jnp.where(where_to >= 0, where_to, total) * block_rows
        for c in range(6):
            send[pl.ds(row + c, 1), :] = shared[pl.ds(c * slots + k, 1), :]
        return carry

    lax.fori_loop(0, slots, pack_shared, 0, unroll=4)
    copy = pltpu.make_async_copy(send.at[pl.ds(0, total * block_rows)], send_out, send_sem)
    copy.start()

    def finish(z, carry):
        store(z).wait()
        return carry

    lax.fori_loop(0, depth, finish, 0)
    copy.wait()


def advect(tiles, rank, rho, flow, kelvin, own, received, shared):
    depth, height, width = rho.shape
    total = tiles.shape[1]
    return pl.pallas_call(
        advect_kernel,
        out_shape=(
            struct(fields, depth, height, width),
            struct(total * block_rows, width),
        ),
        in_specs=[smem_spec] * 2 + [any_spec] * 3 + [vmem_spec] * 7,
        out_specs=(any_spec,) * 2,
        scratch_shapes=[
            VM((fields, depth, height + 2 * row_pad, width), jnp.float32),
            VM((fields, depth * height, width), jnp.float32),
            VM(((total + 2) * block_rows, width), jnp.float32),
            VM((fields, height, width), jnp.float32),
            VM((fields, height + row_pad, width), jnp.float32),
            VM((2 * fields, height, width), jnp.float32),
            pltpu.SemaphoreType.DMA((3, depth)),
            pltpu.SemaphoreType.DMA((depth,)),
            pltpu.SemaphoreType.DMA,
        ],
        cost_estimate=pl.CostEstimate(
            flops=4_000_000_000, bytes_accessed=12_000_000, transcendentals=0
        ),
        compiler_params=params(32),
        name="advect",
    )(tiles, rank, rho, flow, kelvin, *own, *received, shared)


def mixed(density, gas, sums):
    by_flow = 1.0 / (density + sums[4])
    by_heat = 1.0 / (density + sums[5])
    flow = [(density * gas[c] + sums[c]) * by_flow for c in range(3)]
    return flow + [(density * gas[3] + sums[3]) * by_heat]


def exchange_kernel(
    tiles,
    rank,
    received,
    sent,
    advanced,
    shared,
    solid,
    gas_out,
    solid_out,
    gas,
    fresh,
    slot_gas,
    in_sems,
    out_sems,
):
    _, depth, height, width = advanced.shape
    cells = depth * height
    total = tiles.shape[1]
    slots = rank.shape[0]

    def load(f):
        return pltpu.make_async_copy(
            advanced.at[f], gas.at[f, pl.ds(0, depth)], in_sems.at[f]
        )

    for f in range(fields):
        load(f).start()

    def store(f):
        return pltpu.make_async_copy(
            gas.at[f, pl.ds(0, depth)], gas_out.at[f], out_sems.at[f]
        )

    def gather(k, live):
        spot = rank[k]
        row = jnp.maximum(spot, 0) * block_rows + gas_row
        for f in range(fields):
            slot_gas[f, pl.ds(k, 1), :] = received[pl.ds(row + f, 1), :]
        return live + jnp.where(spot >= 0, 1, 0)

    live = lax.fori_loop(0, slots, gather, 0, unroll=4)

    part = 32

    def blocks(g, carry):
        first = pl.multiple_of(g * part, part)

        def rows(ref, c):
            return ref[pl.ds(first * block_rows + c, part, stride=block_rows), :]

        result = mixed(
            rows(sent, gas_row),
            [rows(sent, gas_row + 1 + c) for c in range(4)],
            [rows(received, c) for c in range(6)],
        )
        for c in range(4):
            fresh[c, pl.ds(first, part), :] = result[c]
        return carry

    lax.fori_loop(0, total // part, blocks, 0)
    for f in range(fields):
        load(f).wait()
    store(0).start()

    def scatter(i, carry):
        block = tiles[0, i]
        block = jnp.where(block >= 0, block, cells)
        z = block // height
        y = block - z * height
        for c in range(4):
            gas[1 + c, z, pl.ds(y, 1), :] = fresh[c, pl.ds(i, 1), :]
        return carry

    lax.fori_loop(0, total, scatter, 0, unroll=8)
    for f in range(1, fields):
        store(f).start()

    result = mixed(
        slot_gas[0],
        [slot_gas[1 + c] for c in range(4)],
        [shared[c * slots : (c + 1) * slots, :] for c in range(6)],
    )
    alive = lax.broadcasted_iota(jnp.int32, (slots, width), 0) < live
    for m in range(2):
        for c in range(4):
            scale = solid[(m * 6 + 4 + c // 3) * slots : (m * 6 + 5 + c // 3) * slots, :]
            base = solid[(m * 6 + c) * slots : (m * 6 + c + 1) * slots, :]
            solid_out[c, pl.ds(m, slots, stride=2), :] = jnp.where(
                alive, base + scale * result[c], 0.0
            )
    for f in range(fields):
        store(f).wait()


def exchange(tiles, rank, received, sent, advanced, shared, solid):
    _, depth, height, width = advanced.shape
    total = tiles.shape[1]
    slots = rank.shape[0]
    return pl.pallas_call(
        exchange_kernel,
        out_shape=(struct(*advanced.shape), struct(4, 2 * slots, width)),
        in_specs=[smem_spec] * 2 + [vmem_spec] * 2 + [any_spec] + [vmem_spec] * 2,
        out_specs=(any_spec, vmem_spec),
        scratch_shapes=[
            VM((fields, depth + 1, height, width), jnp.float32),
            VM((4, total, width), jnp.float32),
            VM((fields, slots, width), jnp.float32),
            pltpu.SemaphoreType.DMA((fields,)),
            pltpu.SemaphoreType.DMA((fields,)),
        ],
        compiler_params=params(32),
        name="exchange",
    )(tiles, rank, received, sent, advanced, shared, solid)


def per_device(
    gaseous_rho,
    gaseous_flow_vector,
    gaseous_kelvin,
    sender_tile_map,
    receiver_arrival_rank,
    bin_active_number,
    grain_inertia,
    grain_motion_vector,
    grain_kelvin,
    grain_voxel_number,
    grain_substance_label,
    exchange_factor,
):
    left, right, low, high = edges(gaseous_rho, gaseous_flow_vector, gaseous_kelvin)

    def shifted(array, axis, step):
        count = lax.axis_size(axis)
        pairs = [(i, i + step) for i in range(count) if 0 <= i + step < count]
        return lax.ppermute(array, axis, pairs)

    received = (
        shifted(right, "gx", 1),
        shifted(left, "gx", -1),
        shifted(high, "gy", 1),
        shifted(low, "gy", -1),
    )
    shared, solid = binning(
        bin_active_number,
        exchange_factor,
        grain_inertia,
        grain_motion_vector,
        grain_kelvin,
        grain_voxel_number,
        grain_substance_label,
    )
    advanced, send = advect(
        sender_tile_map,
        receiver_arrival_rank,
        gaseous_rho,
        gaseous_flow_vector,
        gaseous_kelvin,
        (left, right),
        received,
        shared,
    )
    devices = lax.axis_size("gx") * lax.axis_size("gy")
    width = send.shape[-1]
    arrived = lax.all_to_all(
        send.reshape(devices, -1, width), ("gx", "gy"), split_axis=0, concat_axis=0, tiled=True
    )
    gas_state, solid_state = exchange(
        sender_tile_map,
        receiver_arrival_rank,
        arrived.reshape(-1, width),
        send,
        advanced,
        shared,
        solid,
    )
    return gas_state, solid_state.reshape(4, -1, 2, width)


def solution(mesh):
    placed = (
        P(None, "gy", "gx"),
        P(None, None, "gy", "gx"),
        P(None, "gy", "gx"),
        P(("gx", "gy"), None),
        P(("gx", "gy")),
        P(("gx", "gy")),
        P(("gx", "gy"), None),
        P(None, ("gx", "gy"), None),
        P(("gx", "gy"), None),
        P(("gx", "gy"), None),
        P(("gx", "gy"), None),
        P(),
    )
    return jax.shard_map(
        per_device,
        mesh=mesh,
        in_specs=placed,
        out_specs=(P(None, None, "gy", "gx"), P(None, ("gx", "gy"), None, None)),
        check_vma=False,
    )
```

```python
import functools
import jax
import jax.numpy as jnp
from jax import lax
from jax.experimental import pallas as pl
from jax.experimental.pallas import tpu as pltpu
from jax.sharding import PartitionSpec as P

step_ratio = 0.08
fields = 5
lanes = 128
row_pad = 8
block_rows = 11
gas_row = 6
row_chunk = 16

VM = pltpu.VMEM
vmem_spec = pl.BlockSpec(memory_space=pltpu.VMEM)
smem_spec = pl.BlockSpec(memory_space=pltpu.SMEM)
any_spec = pl.BlockSpec(memory_space=pl.ANY)
hbm_spec = pl.BlockSpec(memory_space=pltpu.HBM)


def params(mib):
    return pltpu.CompilerParams(vmem_limit_bytes=mib * 1024 * 1024)


def struct(*shape):
    return jax.ShapeDtypeStruct(shape, jnp.float32)


def near(*shape):
    return pltpu.VMEM(shape, jnp.float32)


def in_hbm(*arrays):
    return [pltpu.with_memory_space_constraint(a, pltpu.HBM) for a in arrays]


def lane_index(shape):
    return lax.broadcasted_iota(jnp.int32, shape, len(shape) - 1)


def edges_kernel(rho, flow, kelvin, left, right, low, high, held, sems):
    depth, height, _ = rho.shape
    parts = sems.shape[1]
    rows = height // parts

    def copies(part):
        span = pl.ds(part * rows, rows)
        into = pl.ds(row_pad + part * rows, rows)
        return [
            pltpu.make_async_copy(rho.at[:, span], held.at[0, :, into], sems.at[0, part]),
            pltpu.make_async_copy(flow.at[:, :, span], held.at[1:4, :, into], sems.at[1, part]),
            pltpu.make_async_copy(kelvin.at[:, span], held.at[4, :, into], sems.at[2, part]),
        ]

    for part in range(parts):
        for copy in copies(part):
            copy.start()
    lane = lane_index((8, lanes))
    for part in range(parts):
        for copy in copies(part):
            copy.wait()

        def group(g, carry):
            start = pl.multiple_of(part * rows + g * 8, 8)
            span = pl.ds(start, 8)
            inside = pl.ds(row_pad + start, 8)
            first = jnp.zeros((8, lanes), jnp.float32)
            last = jnp.zeros((8, lanes), jnp.float32)
            for f in range(fields):
                for z in range(depth):
                    k = f * depth + z
                    turned = pltpu.roll(held[f, z, inside, :], k + 1, 1)
                    last = jnp.where(lane == k, turned, last)
                    first = jnp.where(lane == k + 1, turned, first)
            left[span, :] = pltpu.roll(first, lanes - 1, 1)
            right[span, :] = last
            return carry

        lax.fori_loop(0, rows // 8, group, 0)
    for f in range(fields):
        for z in range(depth):
            k = f * depth + z
            low[k : k + 1, :] = held[f, z, row_pad : row_pad + 1, :]
            high[k : k + 1, :] = held[f, z, row_pad + height - 1 : row_pad + height, :]


def edges(rho, flow, kelvin):
    depth, height, width = rho.shape
    parts = 4
    return pl.pallas_call(
        edges_kernel,
        out_shape=(
            struct(height, width),
            struct(height, width),
            struct(fields * depth, width),
            struct(fields * depth, width),
            near(fields, depth, height + 2 * row_pad, width),
        ),
        in_specs=[hbm_spec] * 3,
        out_specs=(vmem_spec,) * 5,
        scratch_shapes=[
            pltpu.SemaphoreType.DMA((3, parts)),
        ],
        compiler_params=params(16),
        name="edges",
    )(*in_hbm(rho, flow, kelvin))


def binning_kernel(count, factor, mass, flow, kelvin, cell, label, shared, solid, held, sums):
    slots, padding = mass.shape
    width = lanes

    def group(g, carry):
        span = pl.ds(pl.multiple_of(g * 8, 8), 8)
        base = pl.multiple_of(g * 64, 64)
        for part in range(padding // lanes):
            chunk = pl.ds(part * lanes, lanes)
            m = mass[span, chunk]
            values = [m] + [m * flow[c, span, chunk] for c in range(3)] + [m * kelvin[span, chunk]]
            values = values + [jnp.zeros_like(m)] * 3
            for c in range(8):
                held[part, pl.ds(base + c, 8, stride=8), :] = values[c]
        return carry

    lax.fori_loop(0, slots // 8, group, 0)
    place = lane_index((1, padding))
    columns = lax.broadcasted_iota(jnp.int32, (width, padding), 0)

    def slot_sums(s, carry):
        row = pl.ds(pl.multiple_of(s * 8, 8), 8)
        base = jnp.concatenate([held[part, row, :] for part in range(padding // lanes)], 1)
        target = jnp.where(place < count[s], cell[pl.ds(s, 1), :], -1)
        kind = label[pl.ds(s, 1), :]
        table = jnp.where(columns == target, 1.0, 0.0).astype(jnp.bfloat16)
        both = jnp.concatenate(
            [jnp.where(kind == 0, base, 0.0), jnp.where(kind == 1, base, 0.0)], 0
        )
        coarse = both.astype(jnp.bfloat16)
        fine = (both - coarse.astype(jnp.float32)).astype(jnp.bfloat16)
        summed = lax.dot_general(
            jnp.concatenate([coarse, fine], 0),
            table,
            (((1,), (1,)), ((), ())),
            preferred_element_type=jnp.float32,
        )
        sums[pl.ds(pl.multiple_of(s * 16, 16), 16), :] = summed[0:16] + summed[16:32]
        return carry

    lax.fori_loop(0, slots, slot_sums, 0, unroll=4)
    totals = [0.0] * 6
    for m in range(2):
        drag, thermal = factor[m, 0], factor[m, 1]

        def row(c):
            return sums[pl.ds(8 * m + c, slots, stride=16), :]

        inertia = row(0)
        by_drag = 1.0 / (inertia + drag)
        by_heat = 1.0 / (inertia + thermal)
        for c in range(3):
            scaled = row(1 + c) * by_drag
            solid[(m * 6 + c) * slots : (m * 6 + c + 1) * slots, :] = scaled
            totals[c] = totals[c] + drag * scaled
        scaled = row(4) * by_heat
        solid[(m * 6 + 3) * slots : (m * 6 + 4) * slots, :] = scaled
        totals[3] = totals[3] + thermal * scaled
        by_drag = drag * by_drag
        by_heat = thermal * by_heat
        solid[(m * 6 + 4) * slots : (m * 6 + 5) * slots, :] = by_drag
        solid[(m * 6 + 5) * slots : (m * 6 + 6) * slots, :] = by_heat
        totals[4] = totals[4] + by_drag * inertia
        totals[5] = totals[5] + by_heat * inertia
    for c in range(6):
        shared[c * slots : (c + 1) * slots, :] = totals[c]


def binning(count, factor, mass, flow, kelvin, cell, label):
    slots, padding = mass.shape
    return pl.pallas_call(
        binning_kernel,
        out_shape=(struct(6 * slots, lanes), struct(12 * slots, lanes)),
        in_specs=[smem_spec] * 2 + [vmem_spec] * 5,
        out_specs=(vmem_spec,) * 2,
        scratch_shapes=[
            VM((padding // lanes, slots * 8, lanes), jnp.float32),
            VM((slots * 16, lanes), jnp.float32),
        ],
        cost_estimate=pl.CostEstimate(
            flops=4_000_000_000, bytes_accessed=12_000_000, transcendentals=0
        ),
        compiler_params=params(16),
        name="binning",
    )(count, factor, mass, flow, kelvin, cell, label)


def fluxes(a, b, normal, keep=None):
    speed = (0.5 * step_ratio) * (a[normal] + b[normal]) - (2.0 * step_ratio * step_ratio) * (
        b[0] * b[4] - a[0] * a[4]
    ) / (a[0] + b[0])
    if keep is not None:
        speed = speed * keep
    ahead = speed > 0
    chosen = [jnp.where(ahead, u, v) for u, v in zip(a, b)]
    through = speed * chosen[0]
    return [through] + [through * c for c in chosen[1:]]


def quotient(a, b, bound):
    factor = -(-65536 // b)
    assert all(n * factor // 65536 == n // b for n in range(bound))
    return (a * factor) // 65536


def occupied_kernel(
    tiles,
    rank,
    state,
    from_left,
    from_right,
    from_low,
    from_high,
    shared,
    send,
    kept,
    grab,
    edge,
):
    total = tiles.shape[1]
    slots = rank.shape[0]
    depth = state.shape[1]
    height = state.shape[2] - 2 * row_pad
    gx, gy = lax.axis_index("gx"), lax.axis_index("gy")

    def keep(wall):
        return jnp.where(wall, 0.0, 1.0).astype(jnp.float32)

    keep_left = keep(gx == 0)
    keep_right = keep(gx == lax.axis_size("gx") - 1)
    keep_low = keep(gy == 0)
    keep_high = keep(gy == lax.axis_size("gy") - 1)
    layer = lax.broadcasted_iota(jnp.int32, (8, lanes), 0)

    def gather(i, carry):
        block = jnp.maximum(tiles[0, i], 0)
        z = quotient(block, height, depth * height)
        y = block - z * height
        lower, upper = jnp.maximum(z - 1, 0), jnp.minimum(z + 1, depth - 1)
        at_low = layer == jnp.where(y == 0, 0, -1)
        at_high = layer == jnp.where(y == height - 1, 2, -1)
        for f in range(fields):
            k = f * depth + z
            tile = jnp.where(
                layer < 3,
                state[f, z, pl.ds(y + row_pad - 1, 8), :],
                jnp.where(
                    layer == 3,
                    state[f, lower, pl.ds(y + row_pad - 3, 8), :],
                    state[f, upper, pl.ds(y + row_pad - 4, 8), :],
                ),
            )
            tile = jnp.where(at_low, from_low[pl.ds(k, 1), :], tile)
            tile = jnp.where(at_high, from_high[pl.ds(k, 1), :], tile)
            if f == 0:
                tile = jnp.where(layer == 5, from_left[pl.ds(y, 1), :], tile)
                tile = jnp.where(layer == 6, from_right[pl.ds(y, 1), :], tile)
                tile = jnp.where(layer == 7, z.astype(jnp.float32), tile)
            if f == 1:
                tile = jnp.where(layer == 7, y.astype(jnp.float32), tile)
            grab[f, pl.ds(pl.multiple_of(i * 8, 8), 8), :] = tile
        return carry

    lax.fori_loop(0, total, gather, 0, unroll=4)

    source = lax.broadcasted_iota(jnp.int32, (2 * lanes, fields * lanes), 0)
    target = lane_index((2 * lanes, fields * lanes))
    wanted = jnp.where(
        source < lanes, source // depth * lanes, (source - lanes) // depth * lanes + lanes - 1
    )
    chooser = jnp.where(target == wanted, 1.0, 0.0).astype(jnp.bfloat16)
    level = grab[0, pl.ds(7, total, stride=8), :]
    lane = lane_index((total, lanes))
    own = (lane % depth).astype(jnp.float32) == level
    own = own & (lane < fields * depth)
    halo = jnp.concatenate(
        [jnp.where(own, grab[0, pl.ds(5 + c, total, stride=8), :], 0.0) for c in range(2)], 1
    )
    coarse = halo.astype(jnp.bfloat16)
    rest = halo - coarse.astype(jnp.float32)
    middle = rest.astype(jnp.bfloat16)
    fine = (rest - middle.astype(jnp.float32)).astype(jnp.bfloat16)
    edge[...] = (
        jnp.dot(coarse, chooser, preferred_element_type=jnp.float32)
        + jnp.dot(middle, chooser, preferred_element_type=jnp.float32)
        + jnp.dot(fine, chooser, preferred_element_type=jnp.float32)
    )

    part = 16
    lane = lane_index((part, lanes))
    west_keep = jnp.where(lane == 0, keep_left, 1.0)
    east_keep = jnp.where(lane == lanes - 1, keep_right, 1.0)

    def advance(g, carry):
        first = pl.multiple_of(g * part, part)

        def rows(f, k):
            return grab[f, pl.ds(first * 8 + k, part, stride=8), :]

        def states(k):
            return [rows(f, k) for f in range(fields)]

        z, y = rows(0, 7), rows(1, 7)
        here = states(1)
        sides = [
            edge[pl.ds(first, part), f * lanes : (f + 1) * lanes] for f in range(fields)
        ]
        before = [
            jnp.where(lane == 0, s, pltpu.roll(h, 1, 1)) for s, h in zip(sides, here)
        ]
        after = [
            jnp.where(lane == lanes - 1, s, pltpu.roll(h, lanes - 1, 1))
            for s, h in zip(sides, here)
        ]
        change = [0.0] * fields
        for a, b, normal, mask, sign in (
            (states(3), here, 3, jnp.where(z == 0.0, 0.0, 1.0), -1),
            (here, states(4), 3, jnp.where(z == depth - 1.0, 0.0, 1.0), 1),
            (states(0), here, 2, jnp.where(y == 0.0, keep_low, 1.0), -1),
            (here, states(2), 2, jnp.where(y == height - 1.0, keep_high, 1.0), 1),
            (before, here, 1, west_keep, -1),
            (here, after, 1, east_keep, 1),
        ):
            through = fluxes(a, b, normal, mask)
            change = [c + t if sign > 0 else c - t for c, t in zip(change, through)]
        density = here[0] - change[0]
        inverse = 1.0 / density
        for f in range(fields):
            value = density if f == 0 else (here[0] * here[f] - change[f]) * inverse
            send[pl.ds(first * block_rows + gas_row + f, part, stride=block_rows), :] = value
            kept[f, pl.ds(first, part), :] = value
        return carry

    lax.fori_loop(0, total // part, advance, 0)

    def pack_shared(k, carry):
        slot = jnp.where(rank[k] >= 0, k, 0)
        row = rank[slot] * block_rows
        for c in range(6):
            send[pl.ds(row + c, 1), :] = shared[pl.ds(c * slots + slot, 1), :]
        return carry

    lax.fori_loop(0, slots, pack_shared, 0, unroll=8)


def occupied(tiles, rank, state, received, shared):
    total = tiles.shape[1]
    width = state.shape[-1]
    return pl.pallas_call(
        occupied_kernel,
        out_shape=(struct(total * block_rows, width), struct(fields, total, width)),
        in_specs=[smem_spec] * 2 + [vmem_spec] * 6,
        out_specs=(vmem_spec,) * 2,
        scratch_shapes=[
            VM((fields, total * 8, width), jnp.float32),
            VM((total, fields * width), jnp.float32),
        ],
        compiler_params=params(24),
        name="occupied",
    )(tiles, rank, state, *received, shared)


def advect_kernel(
    rho,
    flow,
    kelvin,
    own_left,
    own_right,
    from_left,
    from_right,
    from_low,
    from_high,
    gas_out,
    state,
    gas,
    flux_z,
    flux_y,
    side,
    side_parts,
    edge_flux,
    in_sems,
    out_sems,
):
    depth, height, width = rho.shape
    gx, gy = lax.axis_index("gx"), lax.axis_index("gy")

    def keep(wall):
        return jnp.where(wall, 0.0, 1.0).astype(jnp.float32)

    keep_left = keep(gx == 0)
    keep_right = keep(gx == lax.axis_size("gx") - 1)
    keep_low = keep(gy == 0)
    keep_high = keep(gy == lax.axis_size("gy") - 1)
    inner = pl.ds(row_pad, height)

    def loads(z):
        return [
            pltpu.make_async_copy(rho.at[z], state.at[0, z, inner], in_sems.at[0, z]),
            pltpu.make_async_copy(flow.at[:, z], state.at[1:4, z, inner], in_sems.at[1, z]),
            pltpu.make_async_copy(kelvin.at[z], state.at[4, z, inner], in_sems.at[2, z]),
        ]

    def store(z):
        rows = pl.ds(pl.multiple_of(z * height, 8), height)
        return pltpu.make_async_copy(gas.at[:, rows], gas_out.at[:, z], out_sems.at[z])

    def start_loads(z, carry):
        for copy in loads(z):
            copy.start()
        return carry

    lax.fori_loop(0, depth, start_loads, 0)

    narrow = lane_index((8, lanes))
    keep_sides = jnp.where(narrow < depth, keep_left, keep_right)

    def boundary(g, carry):
        span = pl.ds(pl.multiple_of(g * 8, 8), 8)

        def split(left_faces, right_faces):
            at_left, at_right = left_faces[span, :], right_faces[span, :]
            parts = []
            for f in range(fields):
                one = pltpu.roll(at_left, (lanes - f * depth) % lanes, 1)
                two = pltpu.roll(at_right, (lanes + depth - f * depth) % lanes, 1)
                parts.append(jnp.where(narrow < depth, one, two))
            return parts

        through = fluxes(split(from_left, own_right), split(own_left, from_right), 1, keep_sides)
        for f in range(fields):
            whole = jnp.where(narrow < 2 * depth, through[f], 0.0)
            coarse = whole.astype(jnp.bfloat16).astype(jnp.float32)
            rest = whole - coarse
            middle = rest.astype(jnp.bfloat16).astype(jnp.float32)
            rest = rest - middle
            packed = coarse + pltpu.roll(middle, 2 * depth, 1) + pltpu.roll(rest, 4 * depth, 1)
            side[pl.ds(pl.multiple_of(f * height + g * 8, 8), 8), :] = packed
        return carry

    lax.fori_loop(0, height // 8, boundary, 0)
    side_parts[...] = side[...].astype(jnp.bfloat16)
    part_row = lax.broadcasted_iota(jnp.int32, (lanes, lanes), 0)
    place_row = jnp.where(part_row < 6 * depth, part_row % (2 * depth), -1)
    place_lane = lane_index((lanes, lanes))
    place_row = jnp.where(place_lane == 0, place_row, jnp.where(place_lane == lanes - 1, place_row - depth, -1))

    for f in range(fields):
        flux_z[f] = jnp.zeros((height, width), jnp.float32)
    for copy in loads(0):
        copy.wait()
    lane = lane_index((row_chunk, lanes))

    def plane(z, carry):
        above = jnp.minimum(z + 1, depth - 1)

        @pl.when(z + 1 < depth)
        def _():
            for copy in loads(above):
                copy.wait()

        keep_z = keep(z + 1 == depth)
        place = jnp.where(place_row == z, 1.0, 0.0).astype(jnp.bfloat16)
        edge_flux[...] = jnp.dot(side_parts[...], place, preferred_element_type=jnp.float32)
        for f in range(fields):
            k = f * depth + z
            state[f, z, row_pad - 1 : row_pad, :] = from_low[pl.ds(k, 1), :]
            state[f, z, row_pad + height : row_pad + height + 1, :] = from_high[pl.ds(k, 1), :]

        def faces_y(start, rows):
            a = [state[f, z, pl.ds(row_pad - 1 + start, rows), :] for f in range(fields)]
            b = [state[f, z, pl.ds(row_pad + start, rows), :] for f in range(fields)]
            for f, value in enumerate(fluxes(a, b, 2)):
                flux_y[f, start : start + rows, :] = value

        for start in range(0, height, row_chunk):
            faces_y(start, row_chunk)
        faces_y(height, 1)
        for f in range(fields):
            flux_y[f, 0:1, :] = flux_y[f, 0:1, :] * keep_low
            flux_y[f, height : height + 1, :] = flux_y[f, height : height + 1, :] * keep_high

        for start in range(0, height, row_chunk):
            span = pl.ds(start, row_chunk)
            here = [state[f, z, pl.ds(row_pad + start, row_chunk), :] for f in range(fields)]
            over = [state[f, above, pl.ds(row_pad + start, row_chunk), :] for f in range(fields)]
            up = fluxes(here, over, 3, keep_z)
            change = []
            for f in range(fields):
                change.append(
                    (up[f] - flux_z[f, span, :])
                    + (flux_y[f, pl.ds(start + 1, row_chunk), :] - flux_y[f, span, :])
                )
                flux_z[f, span, :] = up[f]
            before = [pltpu.roll(h, 1, 1) for h in here]
            faces = fluxes(before, here, 1)
            for f in range(fields):
                edge = edge_flux[pl.ds(f * height + start, row_chunk), :]
                face = jnp.where(lane == 0, edge, faces[f])
                after = jnp.where(lane == lanes - 1, edge, pltpu.roll(face, lanes - 1, 1))
                change[f] = change[f] + (after - face)
            density = here[0] - change[0]
            inverse = 1.0 / density
            rows = pl.ds(pl.multiple_of(z * height + start, 8), row_chunk)
            gas[0, rows, :] = density
            for f in range(1, fields):
                gas[f, rows, :] = (here[0] * here[f] - change[f]) * inverse
        store(z).start()
        return carry

    lax.fori_loop(0, depth, plane, 0)

    def finish(z, carry):
        store(z).wait()
        return carry

    lax.fori_loop(0, depth, finish, 0)


def advect(rho, flow, kelvin, own, received):
    depth, height, width = rho.shape
    return pl.pallas_call(
        advect_kernel,
        out_shape=pltpu.HBM((fields, depth, height, width), jnp.float32),
        in_specs=[hbm_spec] * 3 + [vmem_spec] * 6,
        out_specs=hbm_spec,
        scratch_shapes=[
            VM((fields, depth, height + 2 * row_pad, width), jnp.float32),
            VM((fields, depth * height, width), jnp.float32),
            VM((fields, height, width), jnp.float32),
            VM((fields, height + row_pad, width), jnp.float32),
            VM((fields * height, width), jnp.float32),
            VM((fields * height, width), jnp.bfloat16),
            VM((fields * height, width), jnp.float32),
            pltpu.SemaphoreType.DMA((3, depth)),
            pltpu.SemaphoreType.DMA((depth,)),
        ],
        cost_estimate=pl.CostEstimate(
            flops=4_000_000_000, bytes_accessed=12_000_000, transcendentals=0
        ),
        compiler_params=params(24),
        name="advect",
    )(*in_hbm(rho, flow, kelvin), *own, *received)


def mixed(density, gas, sums):
    by_flow = 1.0 / (density + sums[4])
    by_heat = 1.0 / (density + sums[5])
    flow = [(density * gas[c] + sums[c]) * by_flow for c in range(3)]
    return flow + [(density * gas[3] + sums[3]) * by_heat]


def exchange_kernel(
    tiles,
    rank,
    received,
    kept,
    advanced,
    shared,
    solid,
    gas_out,
    solid_out,
    gas,
    fresh,
    slot_gas,
    in_sems,
    out_sems,
):
    _, depth, height, width = gas_out.shape
    cells = depth * height
    total = tiles.shape[1]
    slots = rank.shape[0]
    part = 32

    def load(c):
        return pltpu.make_async_copy(
            advanced.at[1 + c], gas.at[c, pl.ds(0, depth)], in_sems.at[c]
        )

    def store(c):
        return pltpu.make_async_copy(
            gas.at[c, pl.ds(0, depth)], gas_out.at[1 + c], out_sems.at[c]
        )

    for c in range(4):
        load(c).start()

    def blocks(g, carry):
        first = pl.multiple_of(g * part, part)
        span = pl.ds(first, part)
        result = mixed(
            kept[0, span, :],
            [kept[1 + c, span, :] for c in range(4)],
            [received[pl.ds(first * block_rows + c, part, stride=block_rows), :] for c in range(6)],
        )
        for c in range(4):
            fresh[c, span, :] = result[c]
        return carry

    lax.fori_loop(0, total // part, blocks, 0)
    for c in range(4):
        load(c).wait()

    def scatter(i, carry):
        block = tiles[0, i]
        block = jnp.where(block >= 0, block, cells)
        z = quotient(block, height, cells + 1)
        for c in range(4):
            gas[c, z, pl.ds(block - z * height, 1), :] = fresh[c, pl.ds(i, 1), :]
        return carry

    lax.fori_loop(0, total, scatter, 0, unroll=8)
    for c in range(4):
        store(c).start()

    def gather(k, live):
        spot = rank[k]
        row = jnp.maximum(spot, 0) * block_rows + gas_row
        for f in range(fields):
            slot_gas[f, pl.ds(k, 1), :] = received[pl.ds(row + f, 1), :]
        return live + jnp.where(spot >= 0, 1, 0)

    live = lax.fori_loop(0, slots, gather, 0, unroll=4)
    result = mixed(
        slot_gas[0],
        [slot_gas[1 + c] for c in range(4)],
        [shared[c * slots : (c + 1) * slots, :] for c in range(6)],
    )
    alive = lax.broadcasted_iota(jnp.int32, (slots, width), 0) < live
    for m in range(2):
        for c in range(4):
            scale = solid[(m * 6 + 4 + c // 3) * slots : (m * 6 + 5 + c // 3) * slots, :]
            base = solid[(m * 6 + c) * slots : (m * 6 + c + 1) * slots, :]
            solid_out[c, pl.ds(m, slots, stride=2), :] = jnp.where(
                alive, base + scale * result[c], 0.0
            )
    for c in range(4):
        store(c).wait()


def exchange(tiles, rank, received, kept, advanced, shared, solid):
    _, depth, height, width = advanced.shape
    total = tiles.shape[1]
    slots = rank.shape[0]
    return pl.pallas_call(
        exchange_kernel,
        out_shape=(pltpu.HBM(advanced.shape, jnp.float32), struct(4, 2 * slots, width)),
        in_specs=[smem_spec] * 2 + [vmem_spec] * 2 + [hbm_spec] + [vmem_spec] * 2,
        out_specs=(hbm_spec, vmem_spec),
        scratch_shapes=[
            VM((4, depth + 1, height, width), jnp.float32),
            VM((4, total, width), jnp.float32),
            VM((fields, slots, width), jnp.float32),
            pltpu.SemaphoreType.DMA((4,)),
            pltpu.SemaphoreType.DMA((4,)),
        ],
        input_output_aliases={4: 0},
        compiler_params=params(24),
        name="exchange",
    )(tiles, rank, received, kept, *in_hbm(advanced), shared, solid)


def per_device(
    gaseous_rho,
    gaseous_flow_vector,
    gaseous_kelvin,
    sender_tile_map,
    receiver_arrival_rank,
    bin_active_number,
    grain_inertia,
    grain_motion_vector,
    grain_kelvin,
    grain_voxel_number,
    grain_substance_label,
    exchange_factor,
):
    left, right, low, high, state = edges(gaseous_rho, gaseous_flow_vector, gaseous_kelvin)

    def shifted(array, axis, step):
        count = lax.axis_size(axis)
        return lax.ppermute(array, axis, [(i, (i + step) % count) for i in range(count)])

    received = (
        shifted(right, "gx", 1),
        shifted(left, "gx", -1),
        shifted(high, "gy", 1),
        shifted(low, "gy", -1),
    )
    shared, solid = binning(
        bin_active_number,
        exchange_factor,
        grain_inertia,
        grain_motion_vector,
        grain_kelvin,
        grain_voxel_number,
        grain_substance_label,
    )
    send, kept = occupied(sender_tile_map, receiver_arrival_rank, state, received, shared)
    devices = lax.axis_size("gx") * lax.axis_size("gy")
    width = send.shape[-1]
    arrived = lax.all_to_all(
        send.reshape(devices, block_rows, -1, width), ("gx", "gy"), split_axis=0, concat_axis=0, tiled=True
    )
    advanced = advect(
        gaseous_rho, gaseous_flow_vector, gaseous_kelvin, (left, right), received
    )
    gas_state, solid_state = exchange(
        sender_tile_map,
        receiver_arrival_rank,
        arrived.reshape(-1, width),
        kept,
        advanced,
        shared,
        solid,
    )
    return gas_state, solid_state.reshape(4, -1, 2, width)


def solution(mesh):
    placed = (
        P(None, "gy", "gx"),
        P(None, None, "gy", "gx"),
        P(None, "gy", "gx"),
        P(("gx", "gy"), None),
        P(("gx", "gy")),
        P(("gx", "gy")),
        P(("gx", "gy"), None),
        P(None, ("gx", "gy"), None),
        P(("gx", "gy"), None),
        P(("gx", "gy"), None),
        P(("gx", "gy"), None),
        P(),
    )
    return jax.shard_map(
        per_device,
        mesh=mesh,
        in_specs=placed,
        out_specs=(P(None, None, "gy", "gx"), P(None, ("gx", "gy"), None, None)),
        check_vma=False,
    )
```

```python
import functools
import jax
import jax.numpy as jnp
from jax import lax
from jax.experimental import pallas as pl
from jax.experimental.pallas import tpu as pltpu
from jax.sharding import PartitionSpec as P

step_ratio = 0.08
fields = 5
lanes = 128
row_pad = 8
block_rows = 11
gas_row = 6
row_chunk = 16

VM = pltpu.VMEM
vmem_spec = pl.BlockSpec(memory_space=pltpu.VMEM)
smem_spec = pl.BlockSpec(memory_space=pltpu.SMEM)
any_spec = pl.BlockSpec(memory_space=pl.ANY)
hbm_spec = pl.BlockSpec(memory_space=pltpu.HBM)


def params(mib):
    return pltpu.CompilerParams(vmem_limit_bytes=mib * 1024 * 1024)


def struct(*shape):
    return jax.ShapeDtypeStruct(shape, jnp.float32)


def near(*shape):
    return pltpu.VMEM(shape, jnp.float32)


def in_hbm(*arrays):
    return [pltpu.with_memory_space_constraint(a, pltpu.HBM) for a in arrays]


def lane_index(shape):
    return lax.broadcasted_iota(jnp.int32, shape, len(shape) - 1)


def edges_kernel(rho, flow, kelvin, left, right, low, high, held, sems):
    depth, height, _ = rho.shape
    parts = sems.shape[1]
    rows = height // parts

    def copies(part):
        span = pl.ds(part * rows, rows)
        into = pl.ds(row_pad + part * rows, rows)
        return [
            pltpu.make_async_copy(rho.at[:, span], held.at[0, pl.ds(1, depth), into], sems.at[0, part]),
            pltpu.make_async_copy(flow.at[:, :, span], held.at[1:4, pl.ds(1, depth), into], sems.at[1, part]),
            pltpu.make_async_copy(kelvin.at[:, span], held.at[4, pl.ds(1, depth), into], sems.at[2, part]),
        ]

    for part in range(parts):
        for copy in copies(part):
            copy.start()
    lane = lane_index((rows, lanes))
    for part in range(parts):
        for copy in copies(part):
            copy.wait()

        span = pl.ds(part * rows, rows)
        inside = pl.ds(row_pad + part * rows, rows)
        first = jnp.zeros((rows, lanes), jnp.float32)
        last = jnp.zeros((rows, lanes), jnp.float32)
        for f in range(fields):
            for z in range(depth):
                k = f * depth + z
                turned = pltpu.roll(held[f, z + 1, inside, :], k + 1, 1)
                last = jnp.where(lane == k, turned, last)
                first = jnp.where(lane == k + 1, turned, first)
        left[span, :] = pltpu.roll(first, lanes - 1, 1)
        right[span, :] = last
    for f in range(fields):
        for z in range(depth):
            k = f * depth + z
            low[k : k + 1, :] = held[f, z + 1, row_pad : row_pad + 1, :]
            high[k : k + 1, :] = held[f, z + 1, row_pad + height - 1 : row_pad + height, :]
    for f in range(fields):
        sign = -1.0 if f == 3 else 1.0
        held[f, 0] = sign * held[f, 1]
        held[f, depth + 1] = sign * held[f, depth]


def edges(rho, flow, kelvin):
    depth, height, width = rho.shape
    parts = 4
    return pl.pallas_call(
        edges_kernel,
        out_shape=(
            struct(height, width),
            struct(height, width),
            struct(fields * depth, width),
            struct(fields * depth, width),
            near(fields, depth + 2, height + 2 * row_pad, width),
        ),
        in_specs=[hbm_spec] * 3,
        out_specs=(vmem_spec,) * 5,
        scratch_shapes=[
            pltpu.SemaphoreType.DMA((3, parts)),
        ],
        compiler_params=params(16),
        name="edges",
    )(*in_hbm(rho, flow, kelvin))


def binning_kernel(count, factor, mass, flow, kelvin, cell, label, shared, solid, held, sums):
    slots, padding = mass.shape
    width = lanes

    def group(g, carry):
        span = pl.ds(pl.multiple_of(g * 8, 8), 8)
        base = pl.multiple_of(g * 64, 64)
        for part in range(padding // lanes):
            chunk = pl.ds(part * lanes, lanes)
            m = mass[span, chunk]
            values = [m] + [m * flow[c, span, chunk] for c in range(3)] + [m * kelvin[span, chunk]]
            values = values + [jnp.zeros_like(m)] * 3
            for c in range(8):
                held[part, pl.ds(base + c, 8, stride=8), :] = values[c]
        return carry

    lax.fori_loop(0, slots // 8, group, 0)
    place = lane_index((1, padding))
    columns = lax.broadcasted_iota(jnp.int32, (width, padding), 0)

    def slot_sums(s, carry):
        row = pl.ds(pl.multiple_of(s * 8, 8), 8)
        base = jnp.concatenate([held[part, row, :] for part in range(padding // lanes)], 1)
        target = jnp.where(place < count[s], cell[pl.ds(s, 1), :], -1)
        kind = label[pl.ds(s, 1), :]
        table = jnp.where(columns == target, 1.0, 0.0).astype(jnp.bfloat16)
        both = jnp.concatenate(
            [jnp.where(kind == 0, base, 0.0), jnp.where(kind == 1, base, 0.0)], 0
        )
        coarse = both.astype(jnp.bfloat16)
        fine = (both - coarse.astype(jnp.float32)).astype(jnp.bfloat16)
        summed = lax.dot_general(
            jnp.concatenate([coarse, fine], 0),
            table,
            (((1,), (1,)), ((), ())),
            preferred_element_type=jnp.float32,
        )
        sums[pl.ds(pl.multiple_of(s * 16, 16), 16), :] = summed[0:16] + summed[16:32]
        return carry

    lax.fori_loop(0, slots, slot_sums, 0, unroll=32)
    totals = [0.0] * 6
    for m in range(2):
        drag, thermal = factor[m, 0], factor[m, 1]

        def row(c):
            return sums[pl.ds(8 * m + c, slots, stride=16), :]

        inertia = row(0)
        by_drag = 1.0 / (inertia + drag)
        by_heat = 1.0 / (inertia + thermal)
        for c in range(3):
            scaled = row(1 + c) * by_drag
            solid[(m * 6 + c) * slots : (m * 6 + c + 1) * slots, :] = scaled
            totals[c] = totals[c] + drag * scaled
        scaled = row(4) * by_heat
        solid[(m * 6 + 3) * slots : (m * 6 + 4) * slots, :] = scaled
        totals[3] = totals[3] + thermal * scaled
        by_drag = drag * by_drag
        by_heat = thermal * by_heat
        solid[(m * 6 + 4) * slots : (m * 6 + 5) * slots, :] = by_drag
        solid[(m * 6 + 5) * slots : (m * 6 + 6) * slots, :] = by_heat
        totals[4] = totals[4] + by_drag * inertia
        totals[5] = totals[5] + by_heat * inertia
    for c in range(6):
        shared[c * slots : (c + 1) * slots, :] = totals[c]


def binning(count, factor, mass, flow, kelvin, cell, label):
    slots, padding = mass.shape
    return pl.pallas_call(
        binning_kernel,
        out_shape=(struct(6 * slots, lanes), struct(12 * slots, lanes)),
        in_specs=[smem_spec] * 2 + [vmem_spec] * 5,
        out_specs=(vmem_spec,) * 2,
        scratch_shapes=[
            VM((padding // lanes, slots * 8, lanes), jnp.float32),
            VM((slots * 16, lanes), jnp.float32),
        ],
        cost_estimate=pl.CostEstimate(
            flops=4_000_000_000, bytes_accessed=12_000_000, transcendentals=0
        ),
        compiler_params=params(16),
        name="binning",
    )(count, factor, mass, flow, kelvin, cell, label)


def fluxes(a, b, normal, keep=None):
    speed = (0.5 * step_ratio) * (a[normal] + b[normal]) - (2.0 * step_ratio * step_ratio) * (
        b[0] * b[4] - a[0] * a[4]
    ) / (a[0] + b[0])
    if keep is not None:
        speed = speed * keep
    ahead = speed > 0
    chosen = [jnp.where(ahead, u, v) for u, v in zip(a, b)]
    through = speed * chosen[0]
    return [through] + [through * c for c in chosen[1:]]


def quotient(a, b, bound):
    factor = -(-65536 // b)
    assert all(n * factor // 65536 == n // b for n in range(bound))
    return lax.shift_right_logical(a * factor, 16)


def occupied_kernel(
    tiles,
    rank,
    _,
    own_left,
    own_right,
    from_left,
    from_right,
    from_low,
    from_high,
    shared,
    send_out,
    kept,
    state,
    send,
    grab,
    edge,
    west,
    east,
    sems,
):
    total = tiles.shape[1]
    slots = rank.shape[0]
    height = from_left.shape[0]
    depth = from_low.shape[0] // fields
    pitch = height + 2 * row_pad
    gx, gy = lax.axis_index("gx"), lax.axis_index("gy")

    def walled(wall, f, normal, own, other):
        return jnp.where(wall, -own if f == normal else own, other)

    for f in range(fields):
        for z in range(depth):
            k = slice(f * depth + z, f * depth + z + 1)
            row = (z + 1) * pitch + row_pad
            state[f, row - 1 : row, :] = walled(
                gy == 0, f, 2, state[f, row : row + 1, :], from_low[k, :]
            )
            row = row + height - 1
            state[f, row + 1 : row + 2, :] = walled(
                gy == lax.axis_size("gy") - 1, f, 2, state[f, row : row + 1, :], from_high[k, :]
            )
    lane = lane_index((height, lanes))
    sign = jnp.where((lane >= depth) & (lane < 2 * depth), -1.0, 1.0)
    west[...] = jnp.where(gx == 0, sign * own_left[...], from_left[...])
    east[...] = jnp.where(gx == lax.axis_size("gx") - 1, sign * own_right[...], from_right[...])

    assert depth & (depth - 1) == 0
    layer = lax.broadcasted_iota(jnp.int32, (8, lanes), 0)

    def gather(i, carry):
        block = jnp.maximum(tiles[0, i], 0)
        z = quotient(block, height, depth * height)
        y = block - z * height
        base = block + z * (pitch - height) + pitch + row_pad
        for f in range(fields):
            tile = jnp.where(
                layer < 3,
                state[f, pl.ds(base - 1, 8), :],
                jnp.where(
                    layer == 3,
                    state[f, pl.ds(base - pitch - 3, 8), :],
                    state[f, pl.ds(base + pitch - 4, 8), :],
                ),
            )
            if f == 0:
                tile = jnp.where(layer == 5, west[pl.ds(y, 1), :], tile)
                tile = jnp.where(layer == 6, east[pl.ds(y, 1), :], tile)
                tile = jnp.where(layer == 7, z.astype(jnp.float32), tile)
            grab[f, pl.ds(pl.multiple_of(i * 8, 8), 8), :] = tile
        return carry

    lax.fori_loop(0, total, gather, 0, unroll=8)

    source = lax.broadcasted_iota(jnp.int32, (2 * lanes, lanes), 0)
    target = lane_index((2 * lanes, lanes))
    source = jnp.where(
        target == 0, source, jnp.where(target == lanes - 1, source - lanes, -1)
    )
    level = grab[0, pl.ds(7, total, stride=8), :]
    lane = lane_index((total, lanes))
    own = (lane & (depth - 1)).astype(jnp.float32) == level
    own = own & (lane < fields * depth)
    halo = jnp.concatenate(
        [jnp.where(own, grab[0, pl.ds(5 + c, total, stride=8), :], 0.0) for c in range(2)], 1
    )
    coarse = halo.astype(jnp.bfloat16)
    rest = halo - coarse.astype(jnp.float32)
    middle = rest.astype(jnp.bfloat16)
    fine = (rest - middle.astype(jnp.float32)).astype(jnp.bfloat16)
    for f in range(fields):
        here = (source >= f * depth) & (source < (f + 1) * depth)
        chooser = jnp.where(here, 1.0, 0.0).astype(jnp.bfloat16)
        edge[f] = (
            jnp.dot(coarse, chooser, preferred_element_type=jnp.float32)
            + jnp.dot(middle, chooser, preferred_element_type=jnp.float32)
            + jnp.dot(fine, chooser, preferred_element_type=jnp.float32)
        )

    def pack_shared(k, carry):
        slot = jnp.where(rank[k] >= 0, k, 0)
        row = rank[slot] * block_rows
        for c in range(6):
            send[pl.ds(row + c, 1), :] = shared[pl.ds(c * slots + slot, 1), :]
        return carry

    lax.fori_loop(0, slots, pack_shared, 0, unroll=8)

    part = 32

    def copy_out(g):
        span = pl.ds(pl.multiple_of(g * part * block_rows, 8), part * block_rows)
        return pltpu.make_async_copy(send.at[span], send_out.at[span], sems.at[g])

    lane = lane_index((part, lanes))

    def advance(g, carry):
        first = pl.multiple_of(g * part, part)

        def rows(f, k):
            return grab[f, pl.ds(first * 8 + k, part, stride=8), :]

        def states(k):
            return [rows(f, k) for f in range(fields)]

        here = states(1)
        sides = [edge[f, pl.ds(first, part), :] for f in range(fields)]
        before = [
            jnp.where(lane == 0, s, pltpu.roll(h, 1, 1)) for s, h in zip(sides, here)
        ]
        after = [
            jnp.where(lane == lanes - 1, s, pltpu.roll(h, lanes - 1, 1))
            for s, h in zip(sides, here)
        ]
        change = [0.0] * fields
        for a, b, normal, sign in (
            (states(3), here, 3, -1),
            (here, states(4), 3, 1),
            (states(0), here, 2, -1),
            (here, states(2), 2, 1),
            (before, here, 1, -1),
            (here, after, 1, 1),
        ):
            through = fluxes(a, b, normal)
            change = [c + t if sign > 0 else c - t for c, t in zip(change, through)]
        density = here[0] - change[0]
        inverse = 1.0 / density
        for f in range(fields):
            value = density if f == 0 else (here[0] * here[f] - change[f]) * inverse
            send[pl.ds(first * block_rows + gas_row + f, part, stride=block_rows), :] = value
            kept[f, pl.ds(first, part), :] = value
        copy_out(g).start()
        return carry

    lax.fori_loop(0, total // part, advance, 0)

    for g in range(total // part):
        copy_out(g).wait()


def occupied(tiles, rank, state, own, received, shared):
    total = tiles.shape[1]
    width = state.shape[-1]
    height = own[0].shape[0]
    flat = state.reshape(fields, -1, width)
    return pl.pallas_call(
        occupied_kernel,
        out_shape=(
            pltpu.HBM((total * block_rows, width), jnp.float32),
            struct(fields, total, width),
            near(*flat.shape),
        ),
        in_specs=[smem_spec] * 2 + [vmem_spec] * 8,
        out_specs=(hbm_spec, vmem_spec, vmem_spec),
        scratch_shapes=[
            VM((total * block_rows, width), jnp.float32),
            VM((fields, total * 8, width), jnp.float32),
            VM((fields, total, width), jnp.float32),
            VM((height, width), jnp.float32),
            VM((height, width), jnp.float32),
            pltpu.SemaphoreType.DMA((total // 32,)),
        ],
        input_output_aliases={2: 2},
        compiler_params=params(24),
        name="occupied",
    )(
        tiles,
        rank,
        pltpu.with_memory_space_constraint(flat, pltpu.VMEM),
        *own,
        *received,
        shared,
    )[:2]


def advect_kernel(
    rho,
    flow,
    kelvin,
    own_left,
    own_right,
    from_left,
    from_right,
    from_low,
    from_high,
    gas_out,
    state,
    gas,
    flux_z,
    flux_y,
    side,
    side_parts,
    edge_flux,
    in_sems,
    out_sems,
):
    depth, height, width = rho.shape
    gx, gy = lax.axis_index("gx"), lax.axis_index("gy")

    def keep(wall):
        return jnp.where(wall, 0.0, 1.0).astype(jnp.float32)

    keep_left = keep(gx == 0)
    keep_right = keep(gx == lax.axis_size("gx") - 1)
    keep_low = keep(gy == 0)
    keep_high = keep(gy == lax.axis_size("gy") - 1)
    inner = pl.ds(row_pad, height)

    def loads(z):
        return [
            pltpu.make_async_copy(rho.at[z], state.at[0, z, inner], in_sems.at[0, z]),
            pltpu.make_async_copy(flow.at[:, z], state.at[1:4, z, inner], in_sems.at[1, z]),
            pltpu.make_async_copy(kelvin.at[z], state.at[4, z, inner], in_sems.at[2, z]),
        ]

    def store(z):
        rows = pl.ds(pl.multiple_of(z * height, 8), height)
        return pltpu.make_async_copy(gas.at[:, rows], gas_out.at[:, z], out_sems.at[z])

    def start_loads(z, carry):
        for copy in loads(z):
            copy.start()
        return carry

    lax.fori_loop(0, depth, start_loads, 0)

    narrow = lane_index((8, lanes))
    keep_sides = jnp.where(narrow < depth, keep_left, keep_right)

    def boundary(g, carry):
        span = pl.ds(pl.multiple_of(g * 8, 8), 8)

        def split(left_faces, right_faces):
            at_left, at_right = left_faces[span, :], right_faces[span, :]
            parts = []
            for f in range(fields):
                one = pltpu.roll(at_left, (lanes - f * depth) % lanes, 1)
                two = pltpu.roll(at_right, (lanes + depth - f * depth) % lanes, 1)
                parts.append(jnp.where(narrow < depth, one, two))
            return parts

        through = fluxes(split(from_left, own_right), split(own_left, from_right), 1, keep_sides)
        for f in range(fields):
            whole = jnp.where(narrow < 2 * depth, through[f], 0.0)
            coarse = whole.astype(jnp.bfloat16).astype(jnp.float32)
            rest = whole - coarse
            middle = rest.astype(jnp.bfloat16).astype(jnp.float32)
            rest = rest - middle
            packed = coarse + pltpu.roll(middle, 2 * depth, 1) + pltpu.roll(rest, 4 * depth, 1)
            side[pl.ds(pl.multiple_of(f * height + g * 8, 8), 8), :] = packed
        return carry

    lax.fori_loop(0, height // 8, boundary, 0)
    side_parts[...] = side[...].astype(jnp.bfloat16)
    part_row = lax.broadcasted_iota(jnp.int32, (lanes, lanes), 0)
    place_row = jnp.where(part_row < 6 * depth, part_row % (2 * depth), -1)
    place_lane = lane_index((lanes, lanes))
    place_row = jnp.where(place_lane == 0, place_row, jnp.where(place_lane == lanes - 1, place_row - depth, -1))

    for f in range(fields):
        flux_z[f] = jnp.zeros((height, width), jnp.float32)
    for copy in loads(0):
        copy.wait()
    lane = lane_index((row_chunk, lanes))

    def plane(z, carry):
        above = jnp.minimum(z + 1, depth - 1)

        @pl.when(z + 1 < depth)
        def _():
            for copy in loads(above):
                copy.wait()

        keep_z = keep(z + 1 == depth)
        place = jnp.where(place_row == z, 1.0, 0.0).astype(jnp.bfloat16)
        edge_flux[...] = jnp.dot(side_parts[...], place, preferred_element_type=jnp.float32)
        for f in range(fields):
            k = f * depth + z
            state[f, z, row_pad - 1 : row_pad, :] = from_low[pl.ds(k, 1), :]
            state[f, z, row_pad + height : row_pad + height + 1, :] = from_high[pl.ds(k, 1), :]

        def faces_y(start, rows):
            a = [state[f, z, pl.ds(row_pad - 1 + start, rows), :] for f in range(fields)]
            b = [state[f, z, pl.ds(row_pad + start, rows), :] for f in range(fields)]
            for f, value in enumerate(fluxes(a, b, 2)):
                flux_y[f, start : start + rows, :] = value

        for start in range(0, height, row_chunk):
            faces_y(start, row_chunk)
        faces_y(height, 1)
        for f in range(fields):
            flux_y[f, 0:1, :] = flux_y[f, 0:1, :] * keep_low
            flux_y[f, height : height + 1, :] = flux_y[f, height : height + 1, :] * keep_high

        for start in range(0, height, row_chunk):
            span = pl.ds(start, row_chunk)
            here = [state[f, z, pl.ds(row_pad + start, row_chunk), :] for f in range(fields)]
            over = [state[f, above, pl.ds(row_pad + start, row_chunk), :] for f in range(fields)]
            up = fluxes(here, over, 3, keep_z)
            change = []
            for f in range(fields):
                change.append(
                    (up[f] - flux_z[f, span, :])
                    + (flux_y[f, pl.ds(start + 1, row_chunk), :] - flux_y[f, span, :])
                )
                flux_z[f, span, :] = up[f]
            before = [pltpu.roll(h, 1, 1) for h in here]
            faces = fluxes(before, here, 1)
            for f in range(fields):
                edge = edge_flux[pl.ds(f * height + start, row_chunk), :]
                face = jnp.where(lane == 0, edge, faces[f])
                after = jnp.where(lane == lanes - 1, edge, pltpu.roll(face, lanes - 1, 1))
                change[f] = change[f] + (after - face)
            density = here[0] - change[0]
            inverse = 1.0 / density
            rows = pl.ds(pl.multiple_of(z * height + start, 8), row_chunk)
            gas[0, rows, :] = density
            for f in range(1, fields):
                gas[f, rows, :] = (here[0] * here[f] - change[f]) * inverse
        store(z).start()
        return carry

    lax.fori_loop(0, depth, plane, 0)

    def finish(z, carry):
        store(z).wait()
        return carry

    lax.fori_loop(0, depth, finish, 0)


def advect(rho, flow, kelvin, own, received):
    depth, height, width = rho.shape
    return pl.pallas_call(
        advect_kernel,
        out_shape=pltpu.HBM((fields, depth, height, width), jnp.float32),
        in_specs=[hbm_spec] * 3 + [vmem_spec] * 6,
        out_specs=hbm_spec,
        scratch_shapes=[
            VM((fields, depth, height + 2 * row_pad, width), jnp.float32),
            VM((fields, depth * height, width), jnp.float32),
            VM((fields, height, width), jnp.float32),
            VM((fields, height + row_pad, width), jnp.float32),
            VM((fields * height, width), jnp.float32),
            VM((fields * height, width), jnp.bfloat16),
            VM((fields * height, width), jnp.float32),
            pltpu.SemaphoreType.DMA((3, depth)),
            pltpu.SemaphoreType.DMA((depth,)),
        ],
        cost_estimate=pl.CostEstimate(
            flops=4_000_000_000, bytes_accessed=12_000_000, transcendentals=0
        ),
        compiler_params=params(24),
        name="advect",
    )(*in_hbm(rho, flow, kelvin), *own, *received)


def mixed(density, gas, sums):
    by_flow = 1.0 / (density + sums[4])
    by_heat = 1.0 / (density + sums[5])
    flow = [(density * gas[c] + sums[c]) * by_flow for c in range(3)]
    return flow + [(density * gas[3] + sums[3]) * by_heat]


def exchange_kernel(
    tiles,
    rank,
    received,
    kept,
    advanced,
    shared,
    solid,
    gas_out,
    solid_out,
    gas,
    fresh,
    slot_gas,
    in_sems,
    out_sems,
):
    _, depth, height, width = gas_out.shape
    cells = depth * height
    total = tiles.shape[1]
    slots = rank.shape[0]
    part = 32

    def inside(c):
        return gas.at[c, pl.ds(0, cells)].reshape(depth, height, width)

    def load(c):
        return pltpu.make_async_copy(
            advanced.at[1 + c], inside(c), in_sems.at[c]
        )

    def store(c):
        return pltpu.make_async_copy(
            inside(c), gas_out.at[1 + c], out_sems.at[c]
        )

    for c in range(4):
        load(c).start()

    def blocks(g, carry):
        first = pl.multiple_of(g * part, part)
        span = pl.ds(first, part)
        result = mixed(
            kept[0, span, :],
            [kept[1 + c, span, :] for c in range(4)],
            [received[pl.ds(first * block_rows + c, part, stride=block_rows), :] for c in range(6)],
        )
        for c in range(4):
            fresh[c, span, :] = result[c]
        return carry

    lax.fori_loop(0, total // part, blocks, 0)
    for c in range(4):
        load(c).wait()

    def scatter(i, carry):
        block = tiles[0, i]
        block = jnp.where(block >= 0, block, cells)
        for c in range(4):
            gas[c, pl.ds(block, 1), :] = fresh[c, pl.ds(i, 1), :]
        return carry

    lax.fori_loop(0, total, scatter, 0, unroll=8)
    for c in range(4):
        store(c).start()

    def gather(k, live):
        spot = rank[k]
        row = jnp.maximum(spot, 0) * block_rows + gas_row
        for f in range(fields):
            slot_gas[f, pl.ds(k, 1), :] = received[pl.ds(row + f, 1), :]
        return live + jnp.where(spot >= 0, 1, 0)

    live = lax.fori_loop(0, slots, gather, 0, unroll=4)
    result = mixed(
        slot_gas[0],
        [slot_gas[1 + c] for c in range(4)],
        [shared[c * slots : (c + 1) * slots, :] for c in range(6)],
    )
    alive = lax.broadcasted_iota(jnp.int32, (slots, width), 0) < live
    for m in range(2):
        for c in range(4):
            scale = solid[(m * 6 + 4 + c // 3) * slots : (m * 6 + 5 + c // 3) * slots, :]
            base = solid[(m * 6 + c) * slots : (m * 6 + c + 1) * slots, :]
            solid_out[c, pl.ds(m, slots, stride=2), :] = jnp.where(
                alive, base + scale * result[c], 0.0
            )
    for c in range(4):
        store(c).wait()


def exchange(tiles, rank, received, kept, advanced, shared, solid):
    _, depth, height, width = advanced.shape
    total = tiles.shape[1]
    slots = rank.shape[0]
    return pl.pallas_call(
        exchange_kernel,
        out_shape=(pltpu.HBM(advanced.shape, jnp.float32), struct(4, 2 * slots, width)),
        in_specs=[smem_spec] * 2 + [vmem_spec] * 2 + [hbm_spec] + [vmem_spec] * 2,
        out_specs=(hbm_spec, vmem_spec),
        scratch_shapes=[
            VM((4, depth * height + 8, width), jnp.float32),
            VM((4, total, width), jnp.float32),
            VM((fields, slots, width), jnp.float32),
            pltpu.SemaphoreType.DMA((4,)),
            pltpu.SemaphoreType.DMA((4,)),
        ],
        input_output_aliases={4: 0},
        compiler_params=params(24),
        name="exchange",
    )(tiles, rank, received, kept, *in_hbm(advanced), shared, solid)


def per_device(
    gaseous_rho,
    gaseous_flow_vector,
    gaseous_kelvin,
    sender_tile_map,
    receiver_arrival_rank,
    bin_active_number,
    grain_inertia,
    grain_motion_vector,
    grain_kelvin,
    grain_voxel_number,
    grain_substance_label,
    exchange_factor,
):
    left, right, low, high, state = edges(gaseous_rho, gaseous_flow_vector, gaseous_kelvin)

    def shifted(array, axis, step):
        count = lax.axis_size(axis)
        return lax.ppermute(array, axis, [(i, (i + step) % count) for i in range(count)])

    received = (
        shifted(right, "gx", 1),
        shifted(left, "gx", -1),
        shifted(high, "gy", 1),
        shifted(low, "gy", -1),
    )
    shared, solid = binning(
        bin_active_number,
        exchange_factor,
        grain_inertia,
        grain_motion_vector,
        grain_kelvin,
        grain_voxel_number,
        grain_substance_label,
    )
    send, kept = occupied(
        sender_tile_map, receiver_arrival_rank, state, (left, right), received, shared
    )
    devices = lax.axis_size("gx") * lax.axis_size("gy")
    width = send.shape[-1]
    arrived = lax.all_to_all(
        send.reshape(devices, block_rows, -1, width), ("gx", "gy"), split_axis=0, concat_axis=0, tiled=True
    )
    advanced = advect(
        gaseous_rho, gaseous_flow_vector, gaseous_kelvin, (left, right), received
    )
    gas_state, solid_state = exchange(
        sender_tile_map,
        receiver_arrival_rank,
        arrived.reshape(-1, width),
        kept,
        advanced,
        shared,
        solid,
    )
    return gas_state, solid_state.reshape(4, -1, 2, width)


def solution(mesh):
    placed = (
        P(None, "gy", "gx"),
        P(None, None, "gy", "gx"),
        P(None, "gy", "gx"),
        P(("gx", "gy"), None),
        P(("gx", "gy")),
        P(("gx", "gy")),
        P(("gx", "gy"), None),
        P(None, ("gx", "gy"), None),
        P(("gx", "gy"), None),
        P(("gx", "gy"), None),
        P(("gx", "gy"), None),
        P(),
    )
    return jax.shard_map(
        per_device,
        mesh=mesh,
        in_specs=placed,
        out_specs=(P(None, None, "gy", "gx"), P(None, ("gx", "gy"), None, None)),
        check_vma=False,
    )
```

```python
import functools
import jax
import jax.numpy as jnp
from jax import lax
from jax.experimental import pallas as pl
from jax.experimental.pallas import tpu as pltpu
from jax.sharding import PartitionSpec as P

step_ratio = 0.08
fields = 5
lanes = 128
row_pad = 8
block_rows = 11
gas_row = 6
exchange_pieces = 1
group_fields = 2
row_chunk = 16
advance_part = 32

VM = pltpu.VMEM
vmem_spec = pl.BlockSpec(memory_space=pltpu.VMEM)
smem_spec = pl.BlockSpec(memory_space=pltpu.SMEM)
any_spec = pl.BlockSpec(memory_space=pl.ANY)
hbm_spec = pl.BlockSpec(memory_space=pltpu.HBM)


def params(mib):
    return pltpu.CompilerParams(vmem_limit_bytes=mib * 1024 * 1024)


def struct(*shape):
    return jax.ShapeDtypeStruct(shape, jnp.float32)


def near(*shape):
    return pltpu.VMEM(shape, jnp.float32)


def in_hbm(*arrays):
    return [pltpu.with_memory_space_constraint(a, pltpu.HBM) for a in arrays]


def lane_index(shape):
    return lax.broadcasted_iota(jnp.int32, shape, len(shape) - 1)


def is_even(axis):
    return lax.axis_index(axis) % 2 == 0


def swapped(array, axis, second):
    count = lax.axis_size(axis)
    assert count % 2 == 0
    pairs = [(i, i ^ 1) for i in range(count)]
    if second:
        pairs = [((i + 1) % count, (j + 1) % count) for i, j in pairs]
    return lax.ppermute(array, axis, pairs)


def edges_kernel(rho, flow, kelvin, left, right, x_one, x_two, y_one, y_two, held, sems):
    depth, height, _ = rho.shape
    parts = sems.shape[1]
    planes = depth // parts
    rows = 24
    inner = pl.ds(row_pad, height)

    def copies(part):
        span = pl.ds(part * planes, planes)
        into = pl.ds(1 + part * planes, planes)
        return [
            pltpu.make_async_copy(rho.at[span], held.at[0, into, inner], sems.at[0, part]),
            pltpu.make_async_copy(flow.at[:, span], held.at[1:4, into, inner], sems.at[1, part]),
            pltpu.make_async_copy(kelvin.at[span], held.at[4, into, inner], sems.at[2, part]),
        ]

    for part in range(parts):
        for copy in copies(part):
            copy.start()
    lane = lane_index((rows, lanes))
    even_x, even_y = is_even("gx"), is_even("gy")
    for part in range(parts):
        for copy in copies(part):
            copy.wait()
        for start in range(0, height, rows):
            span = pl.ds(start, rows)
            inside = pl.ds(row_pad + start, rows)
            if part == 0:
                first = jnp.zeros((rows, lanes), jnp.float32)
                last = jnp.zeros((rows, lanes), jnp.float32)
            else:
                first, last = left[span, :], right[span, :]
            for f in range(fields):
                for z in range(part * planes, (part + 1) * planes):
                    k = f * depth + z
                    turned = pltpu.roll(held[f, z + 1, inside, :], k + 1, 1)
                    last = jnp.where(lane == k, turned, last)
                    first = jnp.where(lane == k + 1, turned, first)
            if part == parts - 1:
                first = pltpu.roll(first, lanes - 1, 1)
            left[span, :] = first
            right[span, :] = last
            if part == parts - 1:
                x_one[span, :] = jnp.where(even_x, last, first)
                x_two[span, :] = jnp.where(even_x, first, last)
    for f in range(fields):
        for z in range(depth):
            k = f * depth + z
            low = held[f, z + 1, row_pad : row_pad + 1, :]
            high = held[f, z + 1, row_pad + height - 1 : row_pad + height, :]
            y_one[k : k + 1, :] = jnp.where(even_y, high, low)
            y_two[k : k + 1, :] = jnp.where(even_y, low, high)
    for f in range(fields):
        sign = -1.0 if f == 3 else 1.0
        held[f, 0] = sign * held[f, 1]
        held[f, depth + 1] = sign * held[f, depth]


def edges(rho, flow, kelvin):
    depth, height, width = rho.shape
    parts = 4
    return pl.pallas_call(
        edges_kernel,
        out_shape=(
            struct(height, width),
            struct(height, width),
            struct(height, width),
            struct(height, width),
            struct(fields * depth, width),
            struct(fields * depth, width),
            near(fields, depth + 2, height + 2 * row_pad, width),
        ),
        in_specs=[hbm_spec] * 3,
        out_specs=(vmem_spec,) * 7,
        scratch_shapes=[
            pltpu.SemaphoreType.DMA((3, parts)),
        ],
        compiler_params=params(16),
        name="edges",
    )(*in_hbm(rho, flow, kelvin))


def binning_kernel(
    count, factor, rank, mass, flow, kelvin, cell, label, shared, packed, solid, held, sums
):
    slots, padding = mass.shape
    width = lanes

    def group(g, carry):
        span = pl.ds(pl.multiple_of(g * 8, 8), 8)
        base = pl.multiple_of(g * 64, 64)
        for part in range(padding // lanes):
            chunk = pl.ds(part * lanes, lanes)
            m = mass[span, chunk]
            values = [m] + [m * flow[c, span, chunk] for c in range(3)] + [m * kelvin[span, chunk]]
            values = values + [jnp.zeros_like(m)] * 3
            for c in range(8):
                held[part, pl.ds(base + c, 8, stride=8), :] = values[c]
        return carry

    lax.fori_loop(0, slots // 8, group, 0)
    place = lane_index((1, padding))
    columns = lax.broadcasted_iota(jnp.int32, (width, padding), 0)

    def slot_sums(s, carry):
        row = pl.ds(pl.multiple_of(s * 8, 8), 8)
        base = jnp.concatenate([held[part, row, :] for part in range(padding // lanes)], 1)
        target = jnp.where(place < count[s], cell[pl.ds(s, 1), :], -1)
        kind = label[pl.ds(s, 1), :]
        table = jnp.where(columns == target, 1.0, 0.0).astype(jnp.bfloat16)
        both = jnp.concatenate(
            [jnp.where(kind == 0, base, 0.0), jnp.where(kind == 1, base, 0.0)], 0
        )
        coarse = both.astype(jnp.bfloat16)
        fine = (both - coarse.astype(jnp.float32)).astype(jnp.bfloat16)
        summed = lax.dot_general(
            jnp.concatenate([coarse, fine], 0),
            table,
            (((1,), (1,)), ((), ())),
            preferred_element_type=jnp.float32,
        )
        sums[pl.ds(pl.multiple_of(s * 16, 16), 16), :] = summed[0:16] + summed[16:32]
        return carry

    lax.fori_loop(0, slots, slot_sums, 0, unroll=32)
    totals = [0.0] * 6
    for m in range(2):
        drag, thermal = factor[m, 0], factor[m, 1]

        def row(c):
            return sums[pl.ds(8 * m + c, slots, stride=16), :]

        inertia = row(0)
        by_drag = 1.0 / (inertia + drag)
        by_heat = 1.0 / (inertia + thermal)
        for c in range(3):
            scaled = row(1 + c) * by_drag
            solid[(m * 6 + c) * slots : (m * 6 + c + 1) * slots, :] = scaled
            totals[c] = totals[c] + drag * scaled
        scaled = row(4) * by_heat
        solid[(m * 6 + 3) * slots : (m * 6 + 4) * slots, :] = scaled
        totals[3] = totals[3] + thermal * scaled
        by_drag = drag * by_drag
        by_heat = thermal * by_heat
        solid[(m * 6 + 4) * slots : (m * 6 + 5) * slots, :] = by_drag
        solid[(m * 6 + 5) * slots : (m * 6 + 6) * slots, :] = by_heat
        totals[4] = totals[4] + by_drag * inertia
        totals[5] = totals[5] + by_heat * inertia
    for c in range(6):
        shared[c * slots : (c + 1) * slots, :] = totals[c]

    def pack(k, carry):
        slot = jnp.where(rank[k] >= 0, k, 0)
        row = rank[slot]
        for c in range(6):
            packed[c, pl.ds(row, 1), :] = shared[pl.ds(c * slots + slot, 1), :]
        return carry

    lax.fori_loop(0, slots, pack, 0, unroll=16)


def binning(count, factor, rank, total, mass, flow, kelvin, cell, label):
    slots, padding = mass.shape
    return pl.pallas_call(
        binning_kernel,
        out_shape=(
            struct(6 * slots, lanes),
            struct(6, total, lanes),
            struct(12 * slots, lanes),
        ),
        in_specs=[smem_spec] * 3 + [vmem_spec] * 5,
        out_specs=(vmem_spec,) * 3,
        scratch_shapes=[
            VM((padding // lanes, slots * 8, lanes), jnp.float32),
            VM((slots * 16, lanes), jnp.float32),
        ],
        cost_estimate=pl.CostEstimate(
            flops=4_000_000_000, bytes_accessed=12_000_000, transcendentals=0
        ),
        compiler_params=params(16),
        name="binning",
    )(count, factor, rank, mass, flow, kelvin, cell, label)


def fluxes(a, b, normal, keep=None):
    speed = (0.5 * step_ratio) * (a[normal] + b[normal]) - (2.0 * step_ratio * step_ratio) * (
        b[0] * b[4] - a[0] * a[4]
    ) / (a[0] + b[0])
    if keep is not None:
        speed = speed * keep
    ahead = speed > 0
    chosen = [jnp.where(ahead, u, v) for u, v in zip(a, b)]
    through = speed * chosen[0]
    return [through] + [through * c for c in chosen[1:]]


def quotient(a, b, bound):
    factor = -(-65536 // b)
    assert all(n * factor // 65536 == n // b for n in range(bound))
    return lax.shift_right_logical(a * factor, 16)


def occupied_kernel(
    tiles,
    _,
    own_left,
    own_right,
    x_one,
    x_two,
    y_one,
    y_two,
    packed,
    send_out,
    kept,
    state,
    send,
    grab,
    edge,
    west,
    east,
    sems,
):
    total = tiles.shape[1]
    height = own_left.shape[0]
    depth = y_one.shape[0] // fields
    pitch = height + 2 * row_pad
    gx, gy = lax.axis_index("gx"), lax.axis_index("gy")
    even_x, even_y = is_even("gx"), is_even("gy")

    def walled(wall, f, normal, own, other):
        return jnp.where(wall, -own if f == normal else own, other)

    for f in range(fields):
        for z in range(depth):
            k = slice(f * depth + z, f * depth + z + 1)
            row = (z + 1) * pitch + row_pad
            state[f, row - 1 : row, :] = walled(
                gy == 0,
                f,
                2,
                state[f, row : row + 1, :],
                jnp.where(even_y, y_two[k, :], y_one[k, :]),
            )
            row = row + height - 1
            state[f, row + 1 : row + 2, :] = walled(
                gy == lax.axis_size("gy") - 1,
                f,
                2,
                state[f, row : row + 1, :],
                jnp.where(even_y, y_one[k, :], y_two[k, :]),
            )
    lane = lane_index((height, lanes))
    sign = jnp.where((lane >= depth) & (lane < 2 * depth), -1.0, 1.0)
    from_left = jnp.where(even_x, x_two[...], x_one[...])
    from_right = jnp.where(even_x, x_one[...], x_two[...])
    west[...] = jnp.where(gx == 0, sign * own_left[...], from_left)
    east[...] = jnp.where(gx == lax.axis_size("gx") - 1, sign * own_right[...], from_right)

    assert depth & (depth - 1) == 0
    layer = lax.broadcasted_iota(jnp.int32, (8, lanes), 0)

    def gather(i, carry):
        block = jnp.maximum(tiles[0, i], 0)
        z = quotient(block, height, depth * height)
        y = block - z * height
        base = block + z * (pitch - height) + pitch + row_pad
        for f in range(fields):
            tile = jnp.where(
                layer < 3,
                state[f, pl.ds(base - 1, 8), :],
                jnp.where(
                    layer == 3,
                    state[f, pl.ds(base - pitch - 3, 8), :],
                    state[f, pl.ds(base + pitch - 4, 8), :],
                ),
            )
            if f == 0:
                tile = jnp.where(layer == 5, west[pl.ds(y, 1), :], tile)
                tile = jnp.where(layer == 6, east[pl.ds(y, 1), :], tile)
                tile = jnp.where(layer == 7, z.astype(jnp.float32), tile)
            grab[f, pl.ds(pl.multiple_of(i * 8, 8), 8), :] = tile
        return carry

    lax.fori_loop(0, total, gather, 0, unroll=16)

    source = lax.broadcasted_iota(jnp.int32, (2 * lanes, lanes), 0)
    target = lane_index((2 * lanes, lanes))
    source = jnp.where(
        target == 0, source, jnp.where(target == lanes - 1, source - lanes, -1)
    )
    level = grab[0, pl.ds(7, total, stride=8), :]
    lane = lane_index((total, lanes))
    own = (lane & (depth - 1)).astype(jnp.float32) == level
    own = own & (lane < fields * depth)
    halo = jnp.concatenate(
        [jnp.where(own, grab[0, pl.ds(5 + c, total, stride=8), :], 0.0) for c in range(2)], 1
    )
    coarse = halo.astype(jnp.bfloat16)
    fine = (halo - coarse.astype(jnp.float32)).astype(jnp.bfloat16)
    for f in range(fields):
        here = (source >= f * depth) & (source < (f + 1) * depth)
        chooser = jnp.where(here, 1.0, 0.0).astype(jnp.bfloat16)
        edge[f] = jnp.dot(coarse, chooser, preferred_element_type=jnp.float32) + jnp.dot(
            fine, chooser, preferred_element_type=jnp.float32
        )

    part = advance_part

    def copy_out(g):
        span = pl.ds(pl.multiple_of(g * part * block_rows, 8), part * block_rows)
        return pltpu.make_async_copy(send.at[span], send_out.at[span], sems.at[g])

    lane = lane_index((part, lanes))

    def advance(g, carry):
        first = pl.multiple_of(g * part, part)

        def rows(f, k):
            return grab[f, pl.ds(first * 8 + k, part, stride=8), :]

        def states(k):
            return [rows(f, k) for f in range(fields)]

        here = states(1)
        sides = [edge[f, pl.ds(first, part), :] for f in range(fields)]
        before = [
            jnp.where(lane == 0, s, pltpu.roll(h, 1, 1)) for s, h in zip(sides, here)
        ]
        after = [
            jnp.where(lane == lanes - 1, s, pltpu.roll(h, lanes - 1, 1))
            for s, h in zip(sides, here)
        ]
        change = [0.0] * fields
        for a, b, normal, sign in (
            (states(3), here, 3, -1),
            (here, states(4), 3, 1),
            (states(0), here, 2, -1),
            (here, states(2), 2, 1),
            (before, here, 1, -1),
            (here, after, 1, 1),
        ):
            through = fluxes(a, b, normal)
            change = [c + t if sign > 0 else c - t for c, t in zip(change, through)]
        density = here[0] - change[0]
        inverse = 1.0 / density
        for c in range(6):
            send[pl.ds(first * block_rows + c, part, stride=block_rows), :] = packed[
                c, pl.ds(first, part), :
            ]
        for f in range(fields):
            value = density if f == 0 else (here[0] * here[f] - change[f]) * inverse
            send[pl.ds(first * block_rows + gas_row + f, part, stride=block_rows), :] = value
            kept[f, pl.ds(first, part), :] = value
        copy_out(g).start()
        return carry

    lax.fori_loop(0, total // part, advance, 0)

    for g in range(total // part):
        copy_out(g).wait()


def occupied(tiles, state, own, received, packed):
    total = tiles.shape[1]
    width = state.shape[-1]
    height = own[0].shape[0]
    flat = state.reshape(fields, -1, width)
    return pl.pallas_call(
        occupied_kernel,
        out_shape=(
            pltpu.HBM((total * block_rows, width), jnp.float32),
            struct(fields, total, width),
            near(*flat.shape),
        ),
        in_specs=[smem_spec] + [vmem_spec] * 8,
        out_specs=(hbm_spec, vmem_spec, vmem_spec),
        scratch_shapes=[
            VM((total * block_rows, width), jnp.float32),
            VM((fields, total * 8, width), jnp.float32),
            VM((fields, total, width), jnp.float32),
            VM((height, width), jnp.float32),
            VM((height, width), jnp.float32),
            pltpu.SemaphoreType.DMA((total // advance_part,)),
        ],
        input_output_aliases={1: 2},
        compiler_params=params(24),
        name="occupied",
    )(
        tiles,
        pltpu.with_memory_space_constraint(flat, pltpu.VMEM),
        *own,
        *received,
        packed,
    )[:2]


def advect_kernel(
    rho,
    flow,
    kelvin,
    own_left,
    own_right,
    x_one,
    x_two,
    y_one,
    y_two,
    gas_out,
    state,
    gas,
    flux_z,
    flux_y,
    side,
    side_parts,
    edge_flux,
    in_sems,
    out_sems,
):
    depth, height, width = rho.shape
    gx, gy = lax.axis_index("gx"), lax.axis_index("gy")
    even_x, even_y = is_even("gx"), is_even("gy")

    def keep(wall):
        return jnp.where(wall, 0.0, 1.0).astype(jnp.float32)

    keep_left = keep(gx == 0)
    keep_right = keep(gx == lax.axis_size("gx") - 1)
    keep_low = keep(gy == 0)
    keep_high = keep(gy == lax.axis_size("gy") - 1)
    inner = pl.ds(row_pad, height)

    def loads(z):
        return [
            pltpu.make_async_copy(rho.at[z], state.at[0, z, inner], in_sems.at[0, z]),
            pltpu.make_async_copy(flow.at[:, z], state.at[1:4, z, inner], in_sems.at[1, z]),
            pltpu.make_async_copy(kelvin.at[z], state.at[4, z, inner], in_sems.at[2, z]),
        ]

    def store(z):
        rows = pl.ds(pl.multiple_of(z * height, 8), height)
        return pltpu.make_async_copy(gas.at[:, rows], gas_out.at[:, z], out_sems.at[z])

    def start_loads(z, carry):
        for copy in loads(z):
            copy.start()
        return carry

    lax.fori_loop(0, depth, start_loads, 0)

    narrow = lane_index((8, lanes))
    keep_sides = jnp.where(narrow < depth, keep_left, keep_right)

    def boundary(g, carry):
        span = pl.ds(pl.multiple_of(g * 8, 8), 8)

        def split(left_faces, right_faces):
            at_left, at_right = left_faces, right_faces
            parts = []
            for f in range(fields):
                one = pltpu.roll(at_left, (lanes - f * depth) % lanes, 1)
                two = pltpu.roll(at_right, (lanes + depth - f * depth) % lanes, 1)
                parts.append(jnp.where(narrow < depth, one, two))
            return parts

        from_left = jnp.where(even_x, x_two[span, :], x_one[span, :])
        from_right = jnp.where(even_x, x_one[span, :], x_two[span, :])
        through = fluxes(
            split(from_left, own_right[span, :]),
            split(own_left[span, :], from_right),
            1,
            keep_sides,
        )
        for f in range(fields):
            whole = jnp.where(narrow < 2 * depth, through[f], 0.0)
            coarse = whole.astype(jnp.bfloat16).astype(jnp.float32)
            rest = whole - coarse
            middle = rest.astype(jnp.bfloat16).astype(jnp.float32)
            rest = rest - middle
            packed = coarse + pltpu.roll(middle, 2 * depth, 1) + pltpu.roll(rest, 4 * depth, 1)
            side[pl.ds(pl.multiple_of(f * height + g * 8, 8), 8), :] = packed
        return carry

    lax.fori_loop(0, height // 8, boundary, 0)
    side_parts[...] = side[...].astype(jnp.bfloat16)
    part_row = lax.broadcasted_iota(jnp.int32, (lanes, lanes), 0)
    place_row = jnp.where(part_row < 6 * depth, part_row % (2 * depth), -1)
    place_lane = lane_index((lanes, lanes))
    place_row = jnp.where(place_lane == 0, place_row, jnp.where(place_lane == lanes - 1, place_row - depth, -1))

    for f in range(fields):
        flux_z[f] = jnp.zeros((height, width), jnp.float32)
    for copy in loads(0):
        copy.wait()
    lane = lane_index((row_chunk, lanes))

    def plane(z, carry):
        above = jnp.minimum(z + 1, depth - 1)

        @pl.when(z + 1 < depth)
        def _():
            for copy in loads(above):
                copy.wait()

        keep_z = keep(z + 1 == depth)
        place = jnp.where(place_row == z, 1.0, 0.0).astype(jnp.bfloat16)
        edge_flux[...] = jnp.dot(side_parts[...], place, preferred_element_type=jnp.float32)
        for f in range(fields):
            k = f * depth + z
            one, two = y_one[pl.ds(k, 1), :], y_two[pl.ds(k, 1), :]
            state[f, z, row_pad - 1 : row_pad, :] = jnp.where(even_y, two, one)
            state[f, z, row_pad + height : row_pad + height + 1, :] = jnp.where(even_y, one, two)

        def faces_y(start, rows):
            a = [state[f, z, pl.ds(row_pad - 1 + start, rows), :] for f in range(fields)]
            b = [state[f, z, pl.ds(row_pad + start, rows), :] for f in range(fields)]
            for f, value in enumerate(fluxes(a, b, 2)):
                flux_y[f, start : start + rows, :] = value

        for start in range(0, height, row_chunk):
            faces_y(start, row_chunk)
        faces_y(height, 1)
        for f in range(fields):
            flux_y[f, 0:1, :] = flux_y[f, 0:1, :] * keep_low
            flux_y[f, height : height + 1, :] = flux_y[f, height : height + 1, :] * keep_high

        for start in range(0, height, row_chunk):
            span = pl.ds(start, row_chunk)
            here = [state[f, z, pl.ds(row_pad + start, row_chunk), :] for f in range(fields)]
            over = [state[f, above, pl.ds(row_pad + start, row_chunk), :] for f in range(fields)]
            up = fluxes(here, over, 3, keep_z)
            change = []
            for f in range(fields):
                change.append(
                    (up[f] - flux_z[f, span, :])
                    + (flux_y[f, pl.ds(start + 1, row_chunk), :] - flux_y[f, span, :])
                )
                flux_z[f, span, :] = up[f]
            before = [pltpu.roll(h, 1, 1) for h in here]
            faces = fluxes(before, here, 1)
            for f in range(fields):
                edge = edge_flux[pl.ds(f * height + start, row_chunk), :]
                face = jnp.where(lane == 0, edge, faces[f])
                after = jnp.where(lane == lanes - 1, edge, pltpu.roll(face, lanes - 1, 1))
                change[f] = change[f] + (after - face)
            density = here[0] - change[0]
            inverse = 1.0 / density
            rows = pl.ds(pl.multiple_of(z * height + start, 8), row_chunk)
            gas[0, rows, :] = density
            for f in range(1, fields):
                gas[f, rows, :] = (here[0] * here[f] - change[f]) * inverse
        store(z).start()
        return carry

    lax.fori_loop(0, depth, plane, 0)

    def finish(z, carry):
        store(z).wait()
        return carry

    lax.fori_loop(0, depth, finish, 0)


def advect(rho, flow, kelvin, own, received):
    depth, height, width = rho.shape
    return pl.pallas_call(
        advect_kernel,
        out_shape=pltpu.HBM((fields, depth, height, width), jnp.float32),
        in_specs=[hbm_spec] * 3 + [vmem_spec] * 6,
        out_specs=hbm_spec,
        scratch_shapes=[
            VM((fields, depth, height + 2 * row_pad, width), jnp.float32),
            VM((fields, depth * height, width), jnp.float32),
            VM((fields, height, width), jnp.float32),
            VM((fields, height + row_pad, width), jnp.float32),
            VM((fields * height, width), jnp.float32),
            VM((fields * height, width), jnp.bfloat16),
            VM((fields * height, width), jnp.float32),
            pltpu.SemaphoreType.DMA((3, depth)),
            pltpu.SemaphoreType.DMA((depth,)),
        ],
        cost_estimate=pl.CostEstimate(
            flops=4_000_000_000, bytes_accessed=12_000_000, transcendentals=0
        ),
        compiler_params=params(24),
        name="advect",
    )(*in_hbm(rho, flow, kelvin), *own, *received)


def mixed(density, gas, sums):
    by_flow = 1.0 / (density + sums[4])
    by_heat = 1.0 / (density + sums[5])
    flow = [(density * gas[c] + sums[c]) * by_flow for c in range(3)]
    return flow + [(density * gas[3] + sums[3]) * by_heat]


def exchange_kernel(
    tiles,
    rank,
    received,
    kept,
    advanced,
    shared,
    solid,
    gas_out,
    solid_out,
    gas,
    fresh,
    slot_gas,
    in_sems,
    out_sems,
):
    _, depth, height, width = gas_out.shape
    cells = depth * height
    total = tiles.shape[1]
    slots = rank.shape[0]
    part = 32

    pieces = in_sems.shape[1]
    planes = depth // pieces

    def inside(c, p):
        rows = pl.ds(p * planes * height, planes * height)
        return gas.at[c, rows].reshape(planes, height, width)

    def load(c, p):
        return pltpu.make_async_copy(
            advanced.at[1 + c, pl.ds(p * planes, planes)], inside(c, p), in_sems.at[c, p]
        )

    def store(c, p):
        return pltpu.make_async_copy(
            inside(c, p), gas_out.at[1 + c, pl.ds(p * planes, planes)], out_sems.at[c, p]
        )

    for c in range(4):
        for p in range(pieces):
            load(c, p).start()

    def blocks(g, carry):
        first = pl.multiple_of(g * part, part)
        span = pl.ds(first, part)
        result = mixed(
            kept[0, span, :],
            [kept[1 + c, span, :] for c in range(4)],
            [received[pl.ds(first * block_rows + c, part, stride=block_rows), :] for c in range(6)],
        )
        for c in range(4):
            fresh[c, span, :] = result[c]
        return carry

    lax.fori_loop(0, total // part, blocks, 0)
    for pair in range(0, 4, group_fields):
        chosen = range(pair, pair + group_fields)
        for c in chosen:
            for p in range(pieces):
                load(c, p).wait()

        def scatter(i, carry):
            block = tiles[0, i]
            block = jnp.where(block >= 0, block, cells)
            for c in chosen:
                gas[c, pl.ds(block, 1), :] = fresh[c, pl.ds(i, 1), :]
            return carry

        lax.fori_loop(0, total, scatter, 0, unroll=16)
        for c in chosen:
            for p in range(pieces):
                store(c, p).start()

    def gather(k, live):
        spot = rank[k]
        row = jnp.maximum(spot, 0) * block_rows + gas_row
        for f in range(fields):
            slot_gas[f, pl.ds(k, 1), :] = received[pl.ds(row + f, 1), :]
        return live + jnp.where(spot >= 0, 1, 0)

    live = lax.fori_loop(0, slots, gather, 0, unroll=4)
    result = mixed(
        slot_gas[0],
        [slot_gas[1 + c] for c in range(4)],
        [shared[c * slots : (c + 1) * slots, :] for c in range(6)],
    )
    alive = lax.broadcasted_iota(jnp.int32, (slots, width), 0) < live
    for m in range(2):
        for c in range(4):
            scale = solid[(m * 6 + 4 + c // 3) * slots : (m * 6 + 5 + c // 3) * slots, :]
            base = solid[(m * 6 + c) * slots : (m * 6 + c + 1) * slots, :]
            solid_out[c, pl.ds(m, slots, stride=2), :] = jnp.where(
                alive, base + scale * result[c], 0.0
            )
    for c in range(4):
        for p in range(pieces):
            store(c, p).wait()


def exchange(tiles, rank, received, kept, advanced, shared, solid):
    _, depth, height, width = advanced.shape
    total = tiles.shape[1]
    slots = rank.shape[0]
    return pl.pallas_call(
        exchange_kernel,
        out_shape=(pltpu.HBM(advanced.shape, jnp.float32), struct(4, 2 * slots, width)),
        in_specs=[smem_spec] * 2 + [vmem_spec] * 2 + [hbm_spec] + [vmem_spec] * 2,
        out_specs=(hbm_spec, vmem_spec),
        scratch_shapes=[
            VM((4, depth * height + 8, width), jnp.float32),
            VM((4, total, width), jnp.float32),
            VM((fields, slots, width), jnp.float32),
            pltpu.SemaphoreType.DMA((4, exchange_pieces)),
            pltpu.SemaphoreType.DMA((4, exchange_pieces)),
        ],
        input_output_aliases={4: 0},
        compiler_params=params(24),
        name="exchange",
    )(tiles, rank, received, kept, *in_hbm(advanced), shared, solid)


def per_device(
    gaseous_rho,
    gaseous_flow_vector,
    gaseous_kelvin,
    sender_tile_map,
    receiver_arrival_rank,
    bin_active_number,
    grain_inertia,
    grain_motion_vector,
    grain_kelvin,
    grain_voxel_number,
    grain_substance_label,
    exchange_factor,
):
    left, right, x_one, x_two, y_one, y_two, state = edges(
        gaseous_rho, gaseous_flow_vector, gaseous_kelvin
    )
    received = (
        swapped(x_one, "gx", False),
        swapped(x_two, "gx", True),
        swapped(y_one, "gy", False),
        swapped(y_two, "gy", True),
    )
    shared, packed, solid = binning(
        bin_active_number,
        exchange_factor,
        receiver_arrival_rank,
        sender_tile_map.shape[1],
        grain_inertia,
        grain_motion_vector,
        grain_kelvin,
        grain_voxel_number,
        grain_substance_label,
    )
    send, kept = occupied(
        sender_tile_map, state, (left, right), received, packed
    )
    devices = lax.axis_size("gx") * lax.axis_size("gy")
    width = send.shape[-1]
    arrived = lax.all_to_all(
        send.reshape(devices, block_rows, -1, width), ("gx", "gy"), split_axis=0, concat_axis=0, tiled=True
    )
    advanced = advect(
        gaseous_rho, gaseous_flow_vector, gaseous_kelvin, (left, right), received
    )
    gas_state, solid_state = exchange(
        sender_tile_map,
        receiver_arrival_rank,
        arrived.reshape(-1, width),
        kept,
        advanced,
        shared,
        solid,
    )
    return gas_state, solid_state.reshape(4, -1, 2, width)


def solution(mesh):
    placed = (
        P(None, "gy", "gx"),
        P(None, None, "gy", "gx"),
        P(None, "gy", "gx"),
        P(("gx", "gy"), None),
        P(("gx", "gy")),
        P(("gx", "gy")),
        P(("gx", "gy"), None),
        P(None, ("gx", "gy"), None),
        P(("gx", "gy"), None),
        P(("gx", "gy"), None),
        P(("gx", "gy"), None),
        P(),
    )
    return jax.shard_map(
        per_device,
        mesh=mesh,
        in_specs=placed,
        out_specs=(P(None, None, "gy", "gx"), P(None, ("gx", "gy"), None, None)),
        check_vma=False,
    )
```

```python
import functools
import jax
import jax.numpy as jnp
from jax import lax
from jax.experimental import pallas as pl
from jax.experimental.pallas import tpu as pltpu
from jax.sharding import PartitionSpec as P

step_ratio = 0.08
fields = 5
lanes = 128
row_pad = 8
block_rows = 11
gas_row = 6
exchange_pieces = 1
group_fields = 2
row_chunk = 16
advance_part = 32

VM = pltpu.VMEM
vmem_spec = pl.BlockSpec(memory_space=pltpu.VMEM)
smem_spec = pl.BlockSpec(memory_space=pltpu.SMEM)
any_spec = pl.BlockSpec(memory_space=pl.ANY)
hbm_spec = pl.BlockSpec(memory_space=pltpu.HBM)


def params(mib):
    return pltpu.CompilerParams(vmem_limit_bytes=mib * 1024 * 1024)


def struct(*shape):
    return jax.ShapeDtypeStruct(shape, jnp.float32)


def near(*shape):
    return pltpu.VMEM(shape, jnp.float32)


def in_hbm(*arrays):
    return [pltpu.with_memory_space_constraint(a, pltpu.HBM) for a in arrays]


def lane_index(shape):
    return lax.broadcasted_iota(jnp.int32, shape, len(shape) - 1)


def is_even(axis):
    return lax.axis_index(axis) % 2 == 0


def swapped(array, axis, second):
    count = lax.axis_size(axis)
    assert count % 2 == 0
    pairs = [(i, i ^ 1) for i in range(count)]
    if second:
        pairs = [((i + 1) % count, (j + 1) % count) for i, j in pairs]
    return lax.ppermute(array, axis, pairs)


def edges_kernel(rho, flow, kelvin, left, right, x_one, x_two, y_one, y_two, held, sems):
    depth, height, _ = rho.shape
    parts = sems.shape[1]
    planes = depth // parts
    rows = 48
    inner = pl.ds(row_pad, height)

    def copies(part):
        span = pl.ds(part * planes, planes)
        into = pl.ds(1 + part * planes, planes)
        return [
            pltpu.make_async_copy(rho.at[span], held.at[0, into, inner], sems.at[0, part]),
            pltpu.make_async_copy(flow.at[:, span], held.at[1:4, into, inner], sems.at[1, part]),
            pltpu.make_async_copy(kelvin.at[span], held.at[4, into, inner], sems.at[2, part]),
        ]

    for part in range(parts):
        for copy in copies(part):
            copy.start()
    lane = lane_index((rows, lanes))
    even_x, even_y = is_even("gx"), is_even("gy")
    for part in range(parts):
        for copy in copies(part):
            copy.wait()
        for start in range(0, height, rows):
            span = pl.ds(start, rows)
            inside = pl.ds(row_pad + start, rows)
            if part == 0:
                first = jnp.zeros((rows, lanes), jnp.float32)
                last = jnp.zeros((rows, lanes), jnp.float32)
            else:
                first, last = left[span, :], right[span, :]
            for f in range(fields):
                for z in range(part * planes, (part + 1) * planes):
                    k = f * depth + z
                    turned = pltpu.roll(held[f, z + 1, inside, :], k + 1, 1)
                    last = jnp.where(lane == k, turned, last)
                    first = jnp.where(lane == k + 1, turned, first)
            if part == parts - 1:
                first = pltpu.roll(first, lanes - 1, 1)
            left[span, :] = first
            right[span, :] = last
            if part == parts - 1:
                x_one[span, :] = jnp.where(even_x, last, first)
                x_two[span, :] = jnp.where(even_x, first, last)
    for f in range(fields):
        for z in range(depth):
            k = f * depth + z
            low = held[f, z + 1, row_pad : row_pad + 1, :]
            high = held[f, z + 1, row_pad + height - 1 : row_pad + height, :]
            y_one[k : k + 1, :] = jnp.where(even_y, high, low)
            y_two[k : k + 1, :] = jnp.where(even_y, low, high)
    for f in range(fields):
        sign = -1.0 if f == 3 else 1.0
        held[f, 0] = sign * held[f, 1]
        held[f, depth + 1] = sign * held[f, depth]


def edges(rho, flow, kelvin):
    depth, height, width = rho.shape
    parts = 4
    return pl.pallas_call(
        edges_kernel,
        out_shape=(
            struct(height, width),
            struct(height, width),
            struct(height, width),
            struct(height, width),
            struct(fields * depth, width),
            struct(fields * depth, width),
            near(fields, depth + 2, height + 2 * row_pad, width),
        ),
        in_specs=[hbm_spec] * 3,
        out_specs=(vmem_spec,) * 7,
        scratch_shapes=[
            pltpu.SemaphoreType.DMA((3, parts)),
        ],
        compiler_params=params(16),
        name="edges",
    )(*in_hbm(rho, flow, kelvin))


def binning_kernel(
    count, factor, rank, mass, flow, kelvin, cell, label, shared, packed, solid, held, sums
):
    slots, padding = mass.shape
    width = lanes

    def group(g, carry):
        span = pl.ds(pl.multiple_of(g * 8, 8), 8)
        base = pl.multiple_of(g * 64, 64)
        for part in range(padding // lanes):
            chunk = pl.ds(part * lanes, lanes)
            m = mass[span, chunk]
            values = [m] + [m * flow[c, span, chunk] for c in range(3)] + [m * kelvin[span, chunk]]
            values = values + [jnp.zeros_like(m)] * 3
            for c in range(8):
                held[part, pl.ds(base + c, 8, stride=8), :] = values[c]
        return carry

    lax.fori_loop(0, slots // 8, group, 0)
    place = lane_index((1, padding))
    columns = lax.broadcasted_iota(jnp.int32, (width, padding), 0)

    def slot_sums(s, carry):
        row = pl.ds(pl.multiple_of(s * 8, 8), 8)
        base = jnp.concatenate([held[part, row, :] for part in range(padding // lanes)], 1)
        target = jnp.where(place < count[s], cell[pl.ds(s, 1), :], -1)
        kind = label[pl.ds(s, 1), :]
        table = jnp.where(columns == target, 1.0, 0.0).astype(jnp.bfloat16)
        both = jnp.concatenate(
            [jnp.where(kind == 0, base, 0.0), jnp.where(kind == 1, base, 0.0)], 0
        )
        coarse = both.astype(jnp.bfloat16)
        fine = (both - coarse.astype(jnp.float32)).astype(jnp.bfloat16)
        summed = lax.dot_general(
            jnp.concatenate([coarse, fine], 0),
            table,
            (((1,), (1,)), ((), ())),
            preferred_element_type=jnp.float32,
        )
        sums[pl.ds(pl.multiple_of(s * 16, 16), 16), :] = summed[0:16] + summed[16:32]
        return carry

    lax.fori_loop(0, slots, slot_sums, 0, unroll=64)
    totals = [0.0] * 6
    for m in range(2):
        drag, thermal = factor[m, 0], factor[m, 1]

        def row(c):
            return sums[pl.ds(8 * m + c, slots, stride=16), :]

        inertia = row(0)
        by_drag = 1.0 / (inertia + drag)
        by_heat = 1.0 / (inertia + thermal)
        for c in range(3):
            scaled = row(1 + c) * by_drag
            solid[(m * 6 + c) * slots : (m * 6 + c + 1) * slots, :] = scaled
            totals[c] = totals[c] + drag * scaled
        scaled = row(4) * by_heat
        solid[(m * 6 + 3) * slots : (m * 6 + 4) * slots, :] = scaled
        totals[3] = totals[3] + thermal * scaled
        by_drag = drag * by_drag
        by_heat = thermal * by_heat
        solid[(m * 6 + 4) * slots : (m * 6 + 5) * slots, :] = by_drag
        solid[(m * 6 + 5) * slots : (m * 6 + 6) * slots, :] = by_heat
        totals[4] = totals[4] + by_drag * inertia
        totals[5] = totals[5] + by_heat * inertia
    for c in range(6):
        shared[c * slots : (c + 1) * slots, :] = totals[c]

    def pack(k, carry):
        slot = jnp.where(rank[k] >= 0, k, 0)
        row = rank[slot]
        for c in range(6):
            packed[c, pl.ds(row, 1), :] = shared[pl.ds(c * slots + slot, 1), :]
        return carry

    lax.fori_loop(0, slots, pack, 0, unroll=16)


def binning(count, factor, rank, total, mass, flow, kelvin, cell, label):
    slots, padding = mass.shape
    return pl.pallas_call(
        binning_kernel,
        out_shape=(
            struct(6 * slots, lanes),
            struct(6, total, lanes),
            struct(12 * slots, lanes),
        ),
        in_specs=[smem_spec] * 3 + [vmem_spec] * 5,
        out_specs=(vmem_spec,) * 3,
        scratch_shapes=[
            VM((padding // lanes, slots * 8, lanes), jnp.float32),
            VM((slots * 16, lanes), jnp.float32),
        ],
        cost_estimate=pl.CostEstimate(
            flops=4_000_000_000, bytes_accessed=12_000_000, transcendentals=0
        ),
        compiler_params=params(16),
        name="binning",
    )(count, factor, rank, mass, flow, kelvin, cell, label)


def fluxes(a, b, normal, keep=None):
    speed = (0.5 * step_ratio) * (a[normal] + b[normal]) - (2.0 * step_ratio * step_ratio) * (
        b[0] * b[4] - a[0] * a[4]
    ) / (a[0] + b[0])
    if keep is not None:
        speed = speed * keep
    ahead = speed > 0
    chosen = [jnp.where(ahead, u, v) for u, v in zip(a, b)]
    through = speed * chosen[0]
    return [through] + [through * c for c in chosen[1:]]


def quotient(a, b, bound):
    factor = -(-65536 // b)
    assert all(n * factor // 65536 == n // b for n in range(bound))
    return lax.shift_right_logical(a * factor, 16)


def occupied_kernel(
    tiles,
    _,
    own_left,
    own_right,
    x_one,
    x_two,
    y_one,
    y_two,
    packed,
    send_out,
    kept,
    state,
    send,
    grab,
    edge,
    west,
    east,
    sems,
):
    total = tiles.shape[1]
    height = own_left.shape[0]
    depth = y_one.shape[0] // fields
    pitch = height + 2 * row_pad
    gx, gy = lax.axis_index("gx"), lax.axis_index("gy")
    even_x, even_y = is_even("gx"), is_even("gy")

    def walled(wall, f, normal, own, other):
        return jnp.where(wall, -own if f == normal else own, other)

    for f in range(fields):
        for z in range(depth):
            k = slice(f * depth + z, f * depth + z + 1)
            row = (z + 1) * pitch + row_pad
            state[f, row - 1 : row, :] = walled(
                gy == 0,
                f,
                2,
                state[f, row : row + 1, :],
                jnp.where(even_y, y_two[k, :], y_one[k, :]),
            )
            row = row + height - 1
            state[f, row + 1 : row + 2, :] = walled(
                gy == lax.axis_size("gy") - 1,
                f,
                2,
                state[f, row : row + 1, :],
                jnp.where(even_y, y_one[k, :], y_two[k, :]),
            )
    lane = lane_index((height, lanes))
    sign = jnp.where((lane >= depth) & (lane < 2 * depth), -1.0, 1.0)
    from_left = jnp.where(even_x, x_two[...], x_one[...])
    from_right = jnp.where(even_x, x_one[...], x_two[...])
    west[...] = jnp.where(gx == 0, sign * own_left[...], from_left)
    east[...] = jnp.where(gx == lax.axis_size("gx") - 1, sign * own_right[...], from_right)

    assert depth & (depth - 1) == 0
    layer = lax.broadcasted_iota(jnp.int32, (8, lanes), 0)

    def gather(i, carry):
        block = jnp.maximum(tiles[0, i], 0)
        z = quotient(block, height, depth * height)
        y = block - z * height
        base = block + z * (pitch - height) + pitch + row_pad
        for f in range(fields):
            tile = jnp.where(
                layer < 3,
                state[f, pl.ds(base - 1, 8), :],
                jnp.where(
                    layer == 3,
                    state[f, pl.ds(base - pitch - 3, 8), :],
                    state[f, pl.ds(base + pitch - 4, 8), :],
                ),
            )
            if f == 0:
                tile = jnp.where(layer == 5, west[pl.ds(y, 1), :], tile)
                tile = jnp.where(layer == 6, east[pl.ds(y, 1), :], tile)
                tile = jnp.where(layer == 7, z.astype(jnp.float32), tile)
            grab[f, pl.ds(pl.multiple_of(i * 8, 8), 8), :] = tile
        return carry

    lax.fori_loop(0, total, gather, 0, unroll=16)

    source = lax.broadcasted_iota(jnp.int32, (2 * lanes, lanes), 0)
    target = lane_index((2 * lanes, lanes))
    source = jnp.where(
        target == 0, source, jnp.where(target == lanes - 1, source - lanes, -1)
    )
    level = grab[0, pl.ds(7, total, stride=8), :]
    lane = lane_index((total, lanes))
    own = (lane & (depth - 1)).astype(jnp.float32) == level
    own = own & (lane < fields * depth)
    halo = jnp.concatenate(
        [jnp.where(own, grab[0, pl.ds(5 + c, total, stride=8), :], 0.0) for c in range(2)], 1
    )
    coarse = halo.astype(jnp.bfloat16)
    fine = (halo - coarse.astype(jnp.float32)).astype(jnp.bfloat16)
    for f in range(fields):
        here = (source >= f * depth) & (source < (f + 1) * depth)
        chooser = jnp.where(here, 1.0, 0.0).astype(jnp.bfloat16)
        edge[f] = jnp.dot(coarse, chooser, preferred_element_type=jnp.float32) + jnp.dot(
            fine, chooser, preferred_element_type=jnp.float32
        )

    part = advance_part

    def copy_out(g):
        span = pl.ds(pl.multiple_of(g * part * block_rows, 8), part * block_rows)
        return pltpu.make_async_copy(send.at[span], send_out.at[span], sems.at[g])

    lane = lane_index((part, lanes))

    def advance(g, carry):
        first = pl.multiple_of(g * part, part)

        def rows(f, k):
            return grab[f, pl.ds(first * 8 + k, part, stride=8), :]

        def states(k):
            return [rows(f, k) for f in range(fields)]

        here = states(1)
        sides = [edge[f, pl.ds(first, part), :] for f in range(fields)]
        before = [
            jnp.where(lane == 0, s, pltpu.roll(h, 1, 1)) for s, h in zip(sides, here)
        ]
        after = [
            jnp.where(lane == lanes - 1, s, pltpu.roll(h, lanes - 1, 1))
            for s, h in zip(sides, here)
        ]
        change = [0.0] * fields
        for a, b, normal, sign in (
            (states(3), here, 3, -1),
            (here, states(4), 3, 1),
            (states(0), here, 2, -1),
            (here, states(2), 2, 1),
            (before, here, 1, -1),
            (here, after, 1, 1),
        ):
            through = fluxes(a, b, normal)
            change = [c + t if sign > 0 else c - t for c, t in zip(change, through)]
        density = here[0] - change[0]
        inverse = 1.0 / density
        for c in range(6):
            send[pl.ds(first * block_rows + c, part, stride=block_rows), :] = packed[
                c, pl.ds(first, part), :
            ]
        for f in range(fields):
            value = density if f == 0 else (here[0] * here[f] - change[f]) * inverse
            send[pl.ds(first * block_rows + gas_row + f, part, stride=block_rows), :] = value
            kept[f, pl.ds(first, part), :] = value
        copy_out(g).start()
        return carry

    lax.fori_loop(0, total // part, advance, 0)

    for g in range(total // part):
        copy_out(g).wait()


def occupied(tiles, state, own, received, packed):
    total = tiles.shape[1]
    width = state.shape[-1]
    height = own[0].shape[0]
    flat = state.reshape(fields, -1, width)
    return pl.pallas_call(
        occupied_kernel,
        out_shape=(
            pltpu.HBM((total * block_rows, width), jnp.float32),
            struct(fields, total, width),
            near(*flat.shape),
        ),
        in_specs=[smem_spec] + [vmem_spec] * 8,
        out_specs=(hbm_spec, vmem_spec, vmem_spec),
        scratch_shapes=[
            VM((total * block_rows, width), jnp.float32),
            VM((fields, total * 8, width), jnp.float32),
            VM((fields, total, width), jnp.float32),
            VM((height, width), jnp.float32),
            VM((height, width), jnp.float32),
            pltpu.SemaphoreType.DMA((total // advance_part,)),
        ],
        input_output_aliases={1: 2},
        compiler_params=params(24),
        name="occupied",
    )(
        tiles,
        pltpu.with_memory_space_constraint(flat, pltpu.VMEM),
        *own,
        *received,
        packed,
    )[:2]


def advect_kernel(
    rho,
    flow,
    kelvin,
    own_left,
    own_right,
    x_one,
    x_two,
    y_one,
    y_two,
    gas_out,
    state,
    gas,
    flux_z,
    flux_y,
    side,
    side_parts,
    edge_flux,
    in_sems,
    out_sems,
):
    depth, height, width = rho.shape
    gx, gy = lax.axis_index("gx"), lax.axis_index("gy")
    even_x, even_y = is_even("gx"), is_even("gy")

    def keep(wall):
        return jnp.where(wall, 0.0, 1.0).astype(jnp.float32)

    keep_left = keep(gx == 0)
    keep_right = keep(gx == lax.axis_size("gx") - 1)
    keep_low = keep(gy == 0)
    keep_high = keep(gy == lax.axis_size("gy") - 1)
    inner = pl.ds(row_pad, height)

    def loads(z):
        return [
            pltpu.make_async_copy(rho.at[z], state.at[0, z, inner], in_sems.at[0, z]),
            pltpu.make_async_copy(flow.at[:, z], state.at[1:4, z, inner], in_sems.at[1, z]),
            pltpu.make_async_copy(kelvin.at[z], state.at[4, z, inner], in_sems.at[2, z]),
        ]

    def store(z):
        rows = pl.ds(pl.multiple_of(z * height, 8), height)
        return pltpu.make_async_copy(gas.at[:, rows], gas_out.at[:, z], out_sems.at[z])

    def start_loads(z, carry):
        for copy in loads(z):
            copy.start()
        return carry

    lax.fori_loop(0, depth, start_loads, 0)

    narrow = lane_index((8, lanes))
    keep_sides = jnp.where(narrow < depth, keep_left, keep_right)

    def boundary(g, carry):
        span = pl.ds(pl.multiple_of(g * 8, 8), 8)

        def split(left_faces, right_faces):
            at_left, at_right = left_faces, right_faces
            parts = []
            for f in range(fields):
                one = pltpu.roll(at_left, (lanes - f * depth) % lanes, 1)
                two = pltpu.roll(at_right, (lanes + depth - f * depth) % lanes, 1)
                parts.append(jnp.where(narrow < depth, one, two))
            return parts

        from_left = jnp.where(even_x, x_two[span, :], x_one[span, :])
        from_right = jnp.where(even_x, x_one[span, :], x_two[span, :])
        through = fluxes(
            split(from_left, own_right[span, :]),
            split(own_left[span, :], from_right),
            1,
            keep_sides,
        )
        for f in range(fields):
            whole = jnp.where(narrow < 2 * depth, through[f], 0.0)
            coarse = whole.astype(jnp.bfloat16).astype(jnp.float32)
            rest = whole - coarse
            middle = rest.astype(jnp.bfloat16).astype(jnp.float32)
            rest = rest - middle
            packed = coarse + pltpu.roll(middle, 2 * depth, 1) + pltpu.roll(rest, 4 * depth, 1)
            side[pl.ds(pl.multiple_of(f * height + g * 8, 8), 8), :] = packed
        return carry

    lax.fori_loop(0, height // 8, boundary, 0)
    side_parts[...] = side[...].astype(jnp.bfloat16)
    part_row = lax.broadcasted_iota(jnp.int32, (lanes, lanes), 0)
    place_row = jnp.where(part_row < 6 * depth, part_row % (2 * depth), -1)
    place_lane = lane_index((lanes, lanes))
    place_row = jnp.where(place_lane == 0, place_row, jnp.where(place_lane == lanes - 1, place_row - depth, -1))

    for f in range(fields):
        flux_z[f] = jnp.zeros((height, width), jnp.float32)
    for copy in loads(0):
        copy.wait()
    lane = lane_index((row_chunk, lanes))

    def plane(z, carry):
        above = jnp.minimum(z + 1, depth - 1)

        @pl.when(z + 1 < depth)
        def _():
            for copy in loads(above):
                copy.wait()

        keep_z = keep(z + 1 == depth)
        place = jnp.where(place_row == z, 1.0, 0.0).astype(jnp.bfloat16)
        edge_flux[...] = jnp.dot(side_parts[...], place, preferred_element_type=jnp.float32)
        for f in range(fields):
            k = f * depth + z
            one, two = y_one[pl.ds(k, 1), :], y_two[pl.ds(k, 1), :]
            state[f, z, row_pad - 1 : row_pad, :] = jnp.where(even_y, two, one)
            state[f, z, row_pad + height : row_pad + height + 1, :] = jnp.where(even_y, one, two)

        def faces_y(start, rows):
            a = [state[f, z, pl.ds(row_pad - 1 + start, rows), :] for f in range(fields)]
            b = [state[f, z, pl.ds(row_pad + start, rows), :] for f in range(fields)]
            for f, value in enumerate(fluxes(a, b, 2)):
                flux_y[f, start : start + rows, :] = value

        for start in range(0, height, row_chunk):
            faces_y(start, row_chunk)
        faces_y(height, 1)
        for f in range(fields):
            flux_y[f, 0:1, :] = flux_y[f, 0:1, :] * keep_low
            flux_y[f, height : height + 1, :] = flux_y[f, height : height + 1, :] * keep_high

        for start in range(0, height, row_chunk):
            span = pl.ds(start, row_chunk)
            here = [state[f, z, pl.ds(row_pad + start, row_chunk), :] for f in range(fields)]
            over = [state[f, above, pl.ds(row_pad + start, row_chunk), :] for f in range(fields)]
            up = fluxes(here, over, 3, keep_z)
            change = []
            for f in range(fields):
                change.append(
                    (up[f] - flux_z[f, span, :])
                    + (flux_y[f, pl.ds(start + 1, row_chunk), :] - flux_y[f, span, :])
                )
                flux_z[f, span, :] = up[f]
            before = [pltpu.roll(h, 1, 1) for h in here]
            faces = fluxes(before, here, 1)
            for f in range(fields):
                edge = edge_flux[pl.ds(f * height + start, row_chunk), :]
                face = jnp.where(lane == 0, edge, faces[f])
                after = jnp.where(lane == lanes - 1, edge, pltpu.roll(face, lanes - 1, 1))
                change[f] = change[f] + (after - face)
            density = here[0] - change[0]
            inverse = 1.0 / density
            rows = pl.ds(pl.multiple_of(z * height + start, 8), row_chunk)
            gas[0, rows, :] = density
            for f in range(1, fields):
                gas[f, rows, :] = (here[0] * here[f] - change[f]) * inverse
        store(z).start()
        return carry

    lax.fori_loop(0, depth, plane, 0)

    def finish(z, carry):
        store(z).wait()
        return carry

    lax.fori_loop(0, depth, finish, 0)


def advect(rho, flow, kelvin, own, received):
    depth, height, width = rho.shape
    return pl.pallas_call(
        advect_kernel,
        out_shape=pltpu.HBM((fields, depth, height, width), jnp.float32),
        in_specs=[hbm_spec] * 3 + [vmem_spec] * 6,
        out_specs=hbm_spec,
        scratch_shapes=[
            VM((fields, depth, height + 2 * row_pad, width), jnp.float32),
            VM((fields, depth * height, width), jnp.float32),
            VM((fields, height, width), jnp.float32),
            VM((fields, height + row_pad, width), jnp.float32),
            VM((fields * height, width), jnp.float32),
            VM((fields * height, width), jnp.bfloat16),
            VM((fields * height, width), jnp.float32),
            pltpu.SemaphoreType.DMA((3, depth)),
            pltpu.SemaphoreType.DMA((depth,)),
        ],
        cost_estimate=pl.CostEstimate(
            flops=4_000_000_000, bytes_accessed=12_000_000, transcendentals=0
        ),
        compiler_params=params(24),
        name="advect",
    )(*in_hbm(rho, flow, kelvin), *own, *received)


def mixed(density, gas, sums):
    by_flow = 1.0 / (density + sums[4])
    by_heat = 1.0 / (density + sums[5])
    flow = [(density * gas[c] + sums[c]) * by_flow for c in range(3)]
    return flow + [(density * gas[3] + sums[3]) * by_heat]


def exchange_kernel(
    tiles,
    rank,
    received,
    kept,
    advanced,
    shared,
    solid,
    gas_out,
    solid_out,
    gas,
    fresh,
    slot_gas,
    in_sems,
    out_sems,
):
    _, depth, height, width = gas_out.shape
    cells = depth * height
    total = tiles.shape[1]
    slots = rank.shape[0]
    part = 32

    pieces = in_sems.shape[1]
    planes = depth // pieces

    def inside(c, p):
        rows = pl.ds(p * planes * height, planes * height)
        return gas.at[c, rows].reshape(planes, height, width)

    def load(c, p):
        return pltpu.make_async_copy(
            advanced.at[1 + c, pl.ds(p * planes, planes)], inside(c, p), in_sems.at[c, p]
        )

    def store(c, p):
        return pltpu.make_async_copy(
            inside(c, p), gas_out.at[1 + c, pl.ds(p * planes, planes)], out_sems.at[c, p]
        )

    for c in range(4):
        for p in range(pieces):
            load(c, p).start()

    def blocks(g, carry):
        first = pl.multiple_of(g * part, part)
        span = pl.ds(first, part)
        result = mixed(
            kept[0, span, :],
            [kept[1 + c, span, :] for c in range(4)],
            [received[pl.ds(first * block_rows + c, part, stride=block_rows), :] for c in range(6)],
        )
        for c in range(4):
            fresh[c, span, :] = result[c]
        return carry

    lax.fori_loop(0, total // part, blocks, 0)
    for pair in range(0, 4, group_fields):
        chosen = range(pair, pair + group_fields)
        for c in chosen:
            for p in range(pieces):
                load(c, p).wait()

        def scatter(i, carry):
            block = tiles[0, i]
            block = jnp.where(block >= 0, block, cells)
            for c in chosen:
                gas[c, pl.ds(block, 1), :] = fresh[c, pl.ds(i, 1), :]
            return carry

        lax.fori_loop(0, total, scatter, 0, unroll=16)
        for c in chosen:
            for p in range(pieces):
                store(c, p).start()

    def gather(k, live):
        spot = rank[k]
        row = jnp.maximum(spot, 0) * block_rows + gas_row
        for f in range(fields):
            slot_gas[f, pl.ds(k, 1), :] = received[pl.ds(row + f, 1), :]
        return live + jnp.where(spot >= 0, 1, 0)

    live = lax.fori_loop(0, slots, gather, 0, unroll=4)
    result = mixed(
        slot_gas[0],
        [slot_gas[1 + c] for c in range(4)],
        [shared[c * slots : (c + 1) * slots, :] for c in range(6)],
    )
    alive = lax.broadcasted_iota(jnp.int32, (slots, width), 0) < live
    for m in range(2):
        for c in range(4):
            scale = solid[(m * 6 + 4 + c // 3) * slots : (m * 6 + 5 + c // 3) * slots, :]
            base = solid[(m * 6 + c) * slots : (m * 6 + c + 1) * slots, :]
            solid_out[c, pl.ds(m, slots, stride=2), :] = jnp.where(
                alive, base + scale * result[c], 0.0
            )
    for c in range(4):
        for p in range(pieces):
            store(c, p).wait()


def exchange(tiles, rank, received, kept, advanced, shared, solid):
    _, depth, height, width = advanced.shape
    total = tiles.shape[1]
    slots = rank.shape[0]
    return pl.pallas_call(
        exchange_kernel,
        out_shape=(pltpu.HBM(advanced.shape, jnp.float32), struct(4, 2 * slots, width)),
        in_specs=[smem_spec] * 2 + [vmem_spec] * 2 + [hbm_spec] + [vmem_spec] * 2,
        out_specs=(hbm_spec, vmem_spec),
        scratch_shapes=[
            VM((4, depth * height + 8, width), jnp.float32),
            VM((4, total, width), jnp.float32),
            VM((fields, slots, width), jnp.float32),
            pltpu.SemaphoreType.DMA((4, exchange_pieces)),
            pltpu.SemaphoreType.DMA((4, exchange_pieces)),
        ],
        input_output_aliases={4: 0},
        compiler_params=params(24),
        name="exchange",
    )(tiles, rank, received, kept, *in_hbm(advanced), shared, solid)


def per_device(
    gaseous_rho,
    gaseous_flow_vector,
    gaseous_kelvin,
    sender_tile_map,
    receiver_arrival_rank,
    bin_active_number,
    grain_inertia,
    grain_motion_vector,
    grain_kelvin,
    grain_voxel_number,
    grain_substance_label,
    exchange_factor,
):
    left, right, x_one, x_two, y_one, y_two, state = edges(
        gaseous_rho, gaseous_flow_vector, gaseous_kelvin
    )
    received = (
        swapped(x_one, "gx", False),
        swapped(x_two, "gx", True),
        swapped(y_one, "gy", False),
        swapped(y_two, "gy", True),
    )
    shared, packed, solid = binning(
        bin_active_number,
        exchange_factor,
        receiver_arrival_rank,
        sender_tile_map.shape[1],
        grain_inertia,
        grain_motion_vector,
        grain_kelvin,
        grain_voxel_number,
        grain_substance_label,
    )
    send, kept = occupied(
        sender_tile_map, state, (left, right), received, packed
    )
    devices = lax.axis_size("gx") * lax.axis_size("gy")
    width = send.shape[-1]
    arrived = lax.all_to_all(
        send.reshape(devices, block_rows, -1, width), ("gx", "gy"), split_axis=0, concat_axis=0, tiled=True
    )
    advanced = advect(
        gaseous_rho, gaseous_flow_vector, gaseous_kelvin, (left, right), received
    )
    gas_state, solid_state = exchange(
        sender_tile_map,
        receiver_arrival_rank,
        arrived.reshape(-1, width),
        kept,
        advanced,
        shared,
        solid,
    )
    return gas_state, solid_state.reshape(4, -1, 2, width)


def solution(mesh):
    placed = (
        P(None, "gy", "gx"),
        P(None, None, "gy", "gx"),
        P(None, "gy", "gx"),
        P(("gx", "gy"), None),
        P(("gx", "gy")),
        P(("gx", "gy")),
        P(("gx", "gy"), None),
        P(None, ("gx", "gy"), None),
        P(("gx", "gy"), None),
        P(("gx", "gy"), None),
        P(("gx", "gy"), None),
        P(),
    )
    return jax.shard_map(
        per_device,
        mesh=mesh,
        in_specs=placed,
        out_specs=(P(None, None, "gy", "gx"), P(None, ("gx", "gy"), None, None)),
        check_vma=False,
    )
```
